32 devices in a mesh: fsdp: 8 (over z, y), rep: 4 (over x, core).
Axes of the slice: x: 2, y: 2, z: 4, core: 2. Of those that a mesh axis runs over, the one named last changes fastest.
Arguments:
- tokens: bfloat16 [32768, 1024], P(('fsdp', 'rep')), may hold values from -6 to 6
- cotangent: bfloat16 [32768, 1024], P(('fsdp', 'rep')), may hold values from -6 to 6
- doc_ids: int32 [32768], P(('fsdp', 'rep')), may hold values from 0 to 7, as said below
- w_qkv: float32 [1024, 3072], P(('fsdp', 'rep')), may hold values from -0.1875 to 0.1875
- w_out: float32 [1024, 1024], P(('fsdp', 'rep')), may hold values from -0.75 to 0.75
- w_in: float32 [1024, 4096], P(('fsdp', 'rep')), may hold values from -0.1875 to 0.1875
- w_down: float32 [4096, 1024], P(('fsdp', 'rep')), may hold values from -0.09375 to 0.09375
- vectors: float32 [13312], P(('fsdp', 'rep'))
- first_qkv: float32 [1024, 3072], P(('fsdp', 'rep')), may hold values from -0.0002 to 0.0002
- first_out: float32 [1024, 1024], P(('fsdp', 'rep')), may hold values from -0.0002 to 0.0002
- first_in: float32 [1024, 4096], P(('fsdp', 'rep')), may hold values from -0.0002 to 0.0002
- first_down: float32 [4096, 1024], P(('fsdp', 'rep')), may hold values from -0.0002 to 0.0002
- first_vectors: float32 [13312], P(('fsdp', 'rep')), may hold values from -0.0002 to 0.0002
- second_qkv: float32 [1024, 3072], P(('fsdp', 'rep')), may hold values from 1e-09 to 1e-07
- second_out: float32 [1024, 1024], P(('fsdp', 'rep')), may hold values from 1e-09 to 1e-07
- second_in: float32 [1024, 4096], P(('fsdp', 'rep')), may hold values from 1e-10 to 1e-08
- second_down: float32 [4096, 1024], P(('fsdp', 'rep')), may hold values from 1e-09 to 1e-07
- second_vectors: float32 [13312], P(('fsdp', 'rep')), may hold values from 1e-09 to 1e-07
Outputs:
- output: bfloat16 [32768, 1024], P(('fsdp', 'rep'))
- input_grad: float32 [32768, 1024], P(('fsdp', 'rep'))
- grad_norm: float32 [1], replicated
- grad_qkv: float32 [1024, 3072], P(('fsdp', 'rep'))
- grad_out: float32 [1024, 1024], P(('fsdp', 'rep'))
- grad_in: float32 [1024, 4096], P(('fsdp', 'rep'))
- grad_down: float32 [4096, 1024], P(('fsdp', 'rep'))
- grad_vectors: float32 [13312], P(('fsdp', 'rep'))
- new_first_qkv: float32 [1024, 3072], P(('fsdp', 'rep'))
- new_first_out: float32 [1024, 1024], P(('fsdp', 'rep'))
- new_first_in: float32 [1024, 4096], P(('fsdp', 'rep'))
- new_first_down: float32 [4096, 1024], P(('fsdp', 'rep'))
- new_first_vectors: float32 [13312], P(('fsdp', 'rep'))
- new_second_qkv: float32 [1024, 3072], P(('fsdp', 'rep'))
- new_second_out: float32 [1024, 1024], P(('fsdp', 'rep'))
- new_second_in: float32 [1024, 4096], P(('fsdp', 'rep'))
- new_second_down: float32 [4096, 1024], P(('fsdp', 'rep'))
- new_second_vectors: float32 [13312], P(('fsdp', 'rep'))
- change_qkv: float32 [1024, 3072], P(('fsdp', 'rep'))
- change_out: float32 [1024, 1024], P(('fsdp', 'rep'))
- change_in: float32 [1024, 4096], P(('fsdp', 'rep'))
- change_down: float32 [4096, 1024], P(('fsdp', 'rep'))
- change_vectors: float32 [13312], P(('fsdp', 'rep'))
The draws below stay inside these ranges and needn't reach their ends.
Inputs may be any that keep to these rules, and one draw needn't show every extreme that they name: Within each block of 1024 tokens (one device's rows) doc_ids starts at 0 and rises by 0 or 1 from token to token; some block holds 8 documents and some block a single document of 1024 tokens.
All inputs are finite; a program needn't handle non-finite values.
Results may differ from the reference program's by a relative error of at most 0.012.
The reference program's roundings to bfloat16 on the way count: a program that leaves them out, or rounds other values in their place, can miss the bound.
Values may be sent and summed in bfloat16 or wider, within the bound.
No kernel may reach another device: no remote copies, remote signals or barrier semaphores. Data moves between devices by JAX's collectives and lax.ppermute only.
A program may use at most 256 MiB of HBM per device.

```python
import math
import jax
import jax.numpy as jnp
from jax import lax

D = 1024
FF = 4096
HEAD_DIM = 64
ROT = 16
STEPS = 10
TOK_DEV = 1024
DOCS_DEV = 8
TOKENS = 32768
VEC = 13312


def draw_doc_ids(key, part):
    blocks = TOKENS // TOK_DEV
    key_count, key_cut = jax.random.split(key)
    counts = jax.random.randint(key_count, (blocks,), 1, DOCS_DEV + 1)
    index = jnp.arange(blocks)
    counts = jnp.where(index == 0, DOCS_DEV, jnp.where(index == blocks - 1, 1, counts))
    block_keys = jax.random.split(key_cut, blocks)

    def one_block(block_key, count):
        order = jax.random.permutation(block_key, TOK_DEV - 1)
        ranks = jnp.argsort(order)
        cuts = (ranks < count - 1).astype(jnp.int32)
        return jnp.concatenate([jnp.zeros((1,), jnp.int32), jnp.cumsum(cuts).astype(jnp.int32)])
    return jax.vmap(one_block)(block_keys, counts).reshape(TOKENS).astype(jnp.int32)


def draw_vectors(key, part):
    index = jnp.arange(VEC)
    key_noise, key_gain = jax.random.split(key)
    gain_zone = (index >= 5 * D + FF) & (index < 6 * D + FF) | (index >= 7 * D + FF) & (index < 8 * D + FF)
    feature = ((index - (5 * D + FF)) % D).astype(jnp.float32) / float(D)
    noise = 0.3 * jnp.clip(jax.random.normal(key_noise, (VEC,), jnp.float32), -4.0, 4.0)
    ramp = 0.6 + 1.2 * feature
    gains = ramp * jax.random.uniform(key_gain, (VEC,), jnp.float32, 0.7, 1.4)
    return jnp.where(gain_zone, gains, noise).astype(jnp.float32)


def block_scale(key, shape, cuts, least, largest):
    def one(axis_at, shards_of):
        steps = jax.random.uniform(jax.random.fold_in(jax.random.fold_in(key, 6), axis_at), (shards_of,), jnp.float32, least / len(cuts), largest / len(cuts))
        return jnp.repeat(jnp.exp(steps), shape[axis_at] // shards_of).reshape((-1,) + (1,) * (len(shape) - axis_at - 1))

    factor_of = one(*cuts[0])
    for cut in cuts[1:]:
        factor_of = factor_of * one(*cut)
    return factor_of


def centred(stream_key, extent, deviation, bound, shards=(), held_as=jnp.bfloat16):
    values = deviation * jax.random.normal(stream_key, extent, jnp.float32)
    if shards:
        values = values * block_scale(stream_key, extent, shards, -0.22, 0.18)
    return jnp.clip(values, -bound, bound).astype(held_as)


def setup_inputs(seed: int = 0) -> dict:
    splits = jax.random.split(jax.random.key(seed), 19)
    tokens = centred(splits[0], (TOKENS, D), 1.0, 6.0, ((0, 32),))
    cotangent = centred(splits[1], (TOKENS, D), 1.0, 6.0, ((0, 32),))
    doc_ids = draw_doc_ids(jax.random.fold_in(splits[18], 71), 0)
    w_qkv = centred(splits[3], (D, 3 * D), D ** -0.5, 0.1875, ((0, 32),), jnp.float32)
    w_out = centred(splits[4], (D, D), (D // 16) ** -0.5, 0.75, ((0, 32),), jnp.float32)
    w_in = centred(splits[5], (D, FF), D ** -0.5, 0.1875, ((0, 32),), jnp.float32)
    w_down = centred(splits[6], (FF, D), FF ** -0.5, 0.09375, ((0, 32),), jnp.float32)
    vectors = draw_vectors(jax.random.fold_in(splits[18], 71), 0)
    first_qkv = centred(splits[8], (D, 3 * D), 0.00003, 0.0002, ((0, 32),), jnp.float32)
    first_out = centred(splits[9], (D, D), 0.00003, 0.0002, ((0, 32),), jnp.float32)
    first_in = centred(splits[10], (D, FF), 0.00003, 0.0002, ((0, 32),), jnp.float32)
    first_down = centred(splits[11], (FF, D), 0.00003, 0.0002, ((0, 32),), jnp.float32)
    first_vectors = centred(splits[12], (VEC,), 0.00003, 0.0002, ((0, 32),), jnp.float32)
    second_qkv = jnp.clip(jnp.exp(math.log(1.0000000116860974e-07) - 4.6051702 * jax.random.uniform(splits[13], (D, 3 * D), jnp.float32) ** block_scale(splits[13], (D, 3 * D), ((0, 32),), -0.2, 0.2)), 9.999999717180685e-10, 1.0000000116860974e-07)
    second_out = jnp.clip(jnp.exp(math.log(1.0000000116860974e-07) - 4.6051702 * jax.random.uniform(splits[14], (D, D), jnp.float32) ** block_scale(splits[14], (D, D), ((0, 32),), -0.2, 0.2)), 9.999999717180685e-10, 1.0000000116860974e-07)
    second_in = jnp.clip(jnp.exp(math.log(9.99999993922529e-09) - 4.6051702 * jax.random.uniform(splits[15], (D, FF), jnp.float32) ** block_scale(splits[15], (D, FF), ((0, 32),), -0.2, 0.2)), 1.000000013351432e-10, 9.99999993922529e-09)
    second_down = jnp.clip(jnp.exp(math.log(1.0000000116860974e-07) - 4.6051702 * jax.random.uniform(splits[16], (FF, D), jnp.float32) ** block_scale(splits[16], (FF, D), ((0, 32),), -0.2, 0.2)), 9.999999717180685e-10, 1.0000000116860974e-07)
    second_vectors = jnp.clip(jnp.exp(math.log(1.0000000116860974e-07) - 4.6051702 * jax.random.uniform(splits[17], (VEC,), jnp.float32) ** block_scale(splits[17], (VEC,), ((0, 32),), -0.2, 0.2)), 9.999999717180685e-10, 1.0000000116860974e-07)
    return dict(tokens=tokens, cotangent=cotangent, doc_ids=doc_ids, w_qkv=w_qkv, w_out=w_out, w_in=w_in, w_down=w_down, vectors=vectors, first_qkv=first_qkv, first_out=first_out, first_in=first_in, first_down=first_down, first_vectors=first_vectors, second_qkv=second_qkv, second_out=second_out, second_in=second_in, second_down=second_down, second_vectors=second_vectors)


first_decay = 0.9
second_decay = 0.95
adam_eps = 1e-08
weight_decay = 0.1
learn_rate = 0.02
clip_limit = 1.0
norm_eps = 1e-05
highest = lax.Precision.HIGHEST

@jax.custom_vjp
def low(v):
    return lax.optimization_barrier(v.astype(jnp.bfloat16)).astype(jnp.float32)

@jax.custom_vjp
def low_back(v):
    return v

def low_keep(v):
    return (low(v), None)

def low_pass(kept, grad):
    return (grad,)

def back_keep(v):
    return (v, None)

def back_low(kept, grad):
    return (low(grad),)
low.defvjp(low_keep, low_pass)
low_back.defvjp(back_keep, back_low)

def layer_norm(inputs, gain, shift):
    centre = inputs - lax.optimization_barrier(jnp.mean(inputs, axis=-1, keepdims=True))
    spread = lax.optimization_barrier(jnp.mean(centre * centre, axis=-1, keepdims=True))
    return centre * lax.rsqrt(spread + norm_eps) * gain + shift

def positions_of(segments):
    index = jnp.arange(segments.shape[0], dtype=jnp.int32)
    starts = jnp.concatenate([jnp.ones((1,), dtype=bool), segments[1:] != segments[:-1]])
    first = lax.cummax(jnp.where(starts, index, jnp.zeros_like(index)), axis=0)
    return index - first

def rotary_tables(positions):
    half = ROT // 2
    freqs = jnp.exp(jnp.arange(half, dtype=jnp.float32) * (-2.0 * math.log(10000.0) / ROT))
    angles = positions.astype(jnp.float32)[:, None] * freqs[None, :]
    return (jnp.cos(angles)[:, None, :], jnp.sin(angles)[:, None, :])

def rotate_part(heads_in, cosine, sine):
    half = ROT // 2
    lower = heads_in[..., :half]
    upper = heads_in[..., half:ROT]
    return jnp.concatenate([lower * cosine - upper * sine, upper * cosine + lower * sine, heads_in[..., ROT:]], axis=-1)

def split_vector(vector):
    cuts = [3 * D, 4 * D, 4 * D + FF, 5 * D + FF, 6 * D + FF, 7 * D + FF, 8 * D + FF]
    return jnp.split(vector, cuts)

def gelu_exact(values):
    return jax.nn.gelu(values, approximate=False)

def adam_step(weight, grad, first, second, clip, count):
    scaled = grad * clip
    new_first = first_decay * first + (1.0 - first_decay) * scaled
    new_second = second_decay * second + (1.0 - second_decay) * scaled * scaled
    fix_one = 1.0 - first_decay ** count
    fix_two = 1.0 - second_decay ** count
    change = -learn_rate * (new_first / fix_one / (jnp.sqrt(new_second / fix_two) + adam_eps) + weight_decay * weight)
    return (new_first, new_second, change)

def layer_row(inputs, segments, w_qkv, w_out, w_in, w_down, vectors):
    length = inputs.shape[0]
    heads = D // HEAD_DIM
    scale = HEAD_DIM ** (-0.5)
    b_qkv, b_out, b_in, b_down, gain_one, shift_one, gain_two, shift_two = split_vector(low(vectors))
    cosine, sine = rotary_tables(positions_of(segments))
    index = jnp.arange(length, dtype=jnp.int32)
    allowed = (segments[:, None] == segments[None, :]) & (index[:, None] >= index[None, :])
    normed_a = low(layer_norm(inputs, gain_one, shift_one))
    normed_m = low(layer_norm(inputs, gain_two, shift_two))
    joined = low_back(jnp.dot(normed_a, low(w_qkv), precision=highest) + b_qkv).reshape(length, 3, heads, HEAD_DIM)
    queries = low(rotate_part(joined[:, 0], cosine, sine))
    keys_all = low(rotate_part(joined[:, 1], cosine, sine))
    values_all = low(joined[:, 2])

    def one_head(parts):
        query, key_part, value = parts
        scores = low_back(jnp.dot(query, key_part.T, precision=highest) * scale)
        scores = jnp.where(allowed, scores, -1e+30)
        peak = lax.optimization_barrier(jnp.max(scores, axis=-1, keepdims=True))
        weights = jnp.exp(scores - peak)
        probs = weights / lax.optimization_barrier(jnp.sum(weights, axis=-1, keepdims=True))
        return jnp.dot(low(probs), value, precision=highest)
    mixed = lax.map(jax.checkpoint(one_head), (queries.transpose(1, 0, 2), keys_all.transpose(1, 0, 2), values_all.transpose(1, 0, 2)))
    merged = low(low_back(mixed.transpose(1, 0, 2).reshape(length, D)))
    attended = jnp.dot(merged, low(w_out), precision=highest) + b_out
    hidden = low_back(jnp.dot(normed_m, low(w_in), precision=highest) + b_in)
    active = low(gelu_exact(hidden))
    fed = jnp.dot(active, low(w_down), precision=highest) + b_down
    return inputs + attended + fed

def reference(tokens, cotangent, doc_ids, w_qkv, w_out, w_in, w_down, vectors, first_qkv, first_out, first_in, first_down, first_vectors, second_qkv, second_out, second_in, second_down, second_vectors):
    blocks = TOKENS // TOK_DEV
    masters = (w_qkv, w_out, w_in, w_down, vectors)
    rows = (tokens.reshape(blocks, TOK_DEV, D), cotangent.reshape(blocks, TOK_DEV, D), doc_ids.reshape(blocks, TOK_DEV))

    def one_row(totals, row):
        inputs, grad_rows, segments = row

        def forward(values, p_qkv, p_out, p_in, p_down, p_vec):
            return layer_row(values, segments, p_qkv, p_out, p_in, p_down, p_vec)
        result, pull = jax.vjp(forward, inputs.astype(jnp.float32), *masters)
        pulled = pull(grad_rows.astype(jnp.float32))
        new_totals = tuple((total + piece for total, piece in zip(totals, pulled[1:])))
        return (new_totals, (result.astype(jnp.bfloat16), pulled[0]))
    zeros = tuple((jnp.zeros_like(param) for param in masters))
    grads, (outputs, input_grads) = lax.scan(one_row, zeros, rows)
    square = grads[0].sum() * 0.0
    for piece in grads:
        square = square + jnp.sum(piece * piece)
    norm = jnp.sqrt(square)
    clip = jnp.minimum(1.0, clip_limit / (norm + 1e-06))
    count = float(STEPS)
    firsts = (first_qkv, first_out, first_in, first_down, first_vectors)
    seconds = (second_qkv, second_out, second_in, second_down, second_vectors)
    results = [adam_step(w, g, f, s, clip, count) for w, g, f, s in zip(masters, grads, firsts, seconds)]
    return (outputs.reshape(TOKENS, D), input_grads.reshape(TOKENS, D), norm.reshape(1), grads[0], grads[1], grads[2], grads[3], grads[4], results[0][0], results[1][0], results[2][0], results[3][0], results[4][0], results[0][1], results[1][1], results[2][1], results[3][1], results[4][1], results[0][2], results[1][2], results[2][2], results[3][2], results[4][2])
```

```python
import functools
import math

import jax
import jax.numpy as jnp
from jax import lax
from jax.experimental import pallas as pl
from jax.experimental.pallas import tpu as pltpu
from jax.sharding import Mesh
from jax.sharding import PartitionSpec as P

D = 1024
FF = 4096
HEAD_DIM = 64
ROT = 16
STEPS = 10

first_decay = 0.9
second_decay = 0.95
adam_eps = 1e-08
weight_decay = 0.1
learn_rate = 0.02
clip_limit = 1.0
norm_eps = 1e-05

bf16 = jnp.bfloat16
f32 = jnp.float32

HEADS_STEP = 4
WIDTH = HEADS_STEP * HEAD_DIM
QUERY_ROWS = 256
FF_TILE = 512
TOKEN_TILE = 256
HALF = D // 2
VMEM_BYTES = 58 * 2**20


def mul(a, b, dim_a, dim_b):
    return lax.dot_general(a, b, (((dim_a,), (dim_b,)), ((), ())), preferred_element_type=f32)


def positions_of(segments):
    index = jnp.arange(segments.shape[0], dtype=jnp.int32)
    starts = jnp.concatenate([jnp.ones((1,), dtype=bool), segments[1:] != segments[:-1]])
    first = lax.cummax(jnp.where(starts, index, jnp.zeros_like(index)), axis=0)
    return index - first


def split_vector(vector):
    cuts = [3 * D, 4 * D, 4 * D + FF, 5 * D + FF, 6 * D + FF, 7 * D + FF, 8 * D + FF]
    return jnp.split(vector, cuts)


def adam_step(weight, grad, first, second, clip, count):
    scaled = grad * clip
    new_first = first_decay * first + (1.0 - first_decay) * scaled
    new_second = second_decay * second + (1.0 - second_decay) * scaled * scaled
    fix_one = 1.0 - first_decay**count
    fix_two = 1.0 - second_decay**count
    change = -learn_rate * (
        new_first / fix_one / (jnp.sqrt(new_second / fix_two) + adam_eps) + weight_decay * weight
    )
    return (new_first, new_second, change)


def call(kernel, grid, in_specs, out_specs, out_shape, args, after=(), scratch=(), aliases=None, flops=0, moved=0):
    count = len(args)

    def run(*refs):
        kernel(*refs[: 1 + count], *refs[1 + count + len(after) :])

    return pl.pallas_call(
        run,
        grid_spec=pltpu.PrefetchScalarGridSpec(
            num_scalar_prefetch=1,
            grid=grid,
            in_specs=list(in_specs) + [pl.BlockSpec(memory_space=pl.ANY)] * len(after),
            out_specs=list(out_specs),
            scratch_shapes=list(scratch),
        ),
        out_shape=list(out_shape),
        input_output_aliases=aliases or {},
        compiler_params=pltpu.CompilerParams(vmem_limit_bytes=VMEM_BYTES),
        cost_estimate=pl.CostEstimate(flops=flops, bytes_accessed=moved, transcendentals=0),
        name=kernel.__name__,
    )


def whole_block(shape):
    return pl.BlockSpec(shape, lambda g, core: (0,) * len(shape), pipeline_mode=pl.Buffered(1))


def by_core(core, near, far, axis):
    return jnp.where(
        core[0] == 0,
        jnp.concatenate([near, far], axis=axis),
        jnp.concatenate([far, near], axis=axis),
    )


def norm_kernel(core, tokens, gain_one, shift_one, gain_two, shift_two, na, nm, na_t, nm_t):
    inputs = tokens[...].astype(f32)
    centre = inputs - jnp.mean(inputs, axis=-1, keepdims=True)
    spread = jnp.mean(centre * centre, axis=-1, keepdims=True)
    normed = centre * lax.rsqrt(spread + norm_eps)
    one = (normed * gain_one[...] + shift_one[...]).astype(bf16)
    two = (normed * gain_two[...] + shift_two[...]).astype(bf16)
    na[...], nm[...], na_t[...], nm_t[...] = one, two, one.T, two.T


def norms(core, tokens, rows):
    length = tokens.shape[0]
    tile = pl.BlockSpec((TOKEN_TILE, D), lambda g, core: (g, 0))
    turned = pl.BlockSpec((D, TOKEN_TILE), lambda g, core: (0, g))
    sd = jax.ShapeDtypeStruct
    return call(
        norm_kernel, (length // TOKEN_TILE,), [tile] + [whole_block((1, D))] * 4,
        [tile, tile, turned, turned],
        [sd((length, D), bf16)] * 2 + [sd((D, length), bf16)] * 2,
        (tokens,) + rows, flops=10**7, moved=10**7,
    )(core, tokens, *rows)


def attention_kernel(
    core, start, cos, sin, na_t, cot, wq, wk, wv, wo_near, wo_far, bq, bk, bv,
    grads, merged, gq_out, gk_out, gv_out, sum_q, sum_k, sum_v,
    bias, merged_t, gq_t, gk_t, gv_t, acc_k, acc_v,
):
    length = cot.shape[0]
    step = pl.program_id(0)

    @pl.when(step == 0)
    def _():
        key = lax.broadcasted_iota(jnp.int32, (length, length), 0)
        query = lax.broadcasted_iota(jnp.int32, (length, length), 1)
        bias[...] = jnp.where((key >= start[...]) & (key <= query), 0.0, -1e30)

    c, s = cos[...], sin[...]

    def project(w, b):
        return mul(w[...], na_t[...], 0, 0) + b[...]

    def rotate(v, sign):
        rows = []
        for h in range(HEADS_STEP):
            at = h * HEAD_DIM
            lo, hi = v[at : at + 8], v[at + 8 : at + 16]
            rows += [lo * c - sign * (hi * s), hi * c + sign * (lo * s), v[at + 16 : at + HEAD_DIM]]
        return jnp.concatenate(rows, axis=0)

    scale = HEAD_DIM**-0.5
    q_t = rotate(project(wq, bq), 1.0).astype(bf16) * jnp.asarray(scale, bf16)
    k_t = rotate(project(wk, bk), 1.0).astype(bf16)
    v_t = project(wv, bv).astype(bf16)
    gm_t = mul(by_core(core, wo_near[...], wo_far[...], 1), cot[...], 1, 1).astype(bf16)
    k, v = k_t.T, v_t.T
    for h in range(HEADS_STEP):
        hs = slice(h * HEAD_DIM, (h + 1) * HEAD_DIM)
        acc_k[...] = jnp.zeros_like(acc_k)
        acc_v[...] = jnp.zeros_like(acc_v)
        for i in range(length // QUERY_ROWS):
            n = QUERY_ROWS * (i + 1)
            qs = slice(i * QUERY_ROWS, n)
            scores = mul(k[:n, hs], q_t[hs, qs], 1, 0) + bias[:n, qs]
            weights = jnp.exp(scores - jnp.max(scores, axis=0, keepdims=True))
            probs = weights * (1.0 / jnp.sum(weights, axis=0, keepdims=True))
            probs_low = probs.astype(bf16)
            merged_t[hs, qs] = mul(v_t[hs, :n], probs_low, 1, 0).astype(bf16)
            grad_probs = mul(v[:n, hs], gm_t[hs, qs], 1, 0)
            inner = jnp.sum(grad_probs * probs, axis=0, keepdims=True)
            grad_scores = (probs * (grad_probs - inner)).astype(bf16)
            gq_t[hs, qs] = mul(k_t[hs, :n], grad_scores, 1, 0) * scale
            acc_k[:, :n] += mul(q_t[hs, qs], grad_scores, 1, 1)
            acc_v[:, :n] += mul(gm_t[hs, qs], probs_low, 1, 1)
        gk_t[hs, :] = acc_k[...]
        gv_t[hs, :] = acc_v[...]
    gq = rotate(gq_t[...], -1.0).astype(bf16)
    gk = rotate(gk_t[...], -1.0).astype(bf16)
    gv = gv_t[...].astype(bf16)
    column = pl.multiple_of(lax.rem(step, 2) * WIDTH, WIDTH)
    gq_out[...], gk_out[...], gv_out[...] = gq, gk, gv
    merged[pl.ds(column, WIDTH), :] = merged_t[...]
    for at, (part, out) in enumerate(((gq, sum_q), (gk, sum_k), (gv, sum_v))):
        out[...] = jnp.sum(part.astype(f32), axis=1, keepdims=True)
        grads[:, pl.ds(at * HALF + column, WIDTH)] = mul(na_t[...], part, 1, 1).astype(bf16)


def attention(core, last, start, cos, sin, na_t, cot, weights, near, far, bias_qkv):
    length = cot.shape[0]

    def at(core, g):
        return g + 2 * (core[0] if last else 1 - core[0])

    def columns(part):
        return pl.BlockSpec((D, WIDTH), lambda g, core: (0, 2 * part + g))

    def entries(part):
        return pl.BlockSpec((WIDTH, 1), lambda g, core: (4 * part + at(core, g), 0))

    sd = jax.ShapeDtypeStruct
    rows_of_out = pl.BlockSpec((WIDTH, HALF), lambda g, core: (at(core, g), 3))
    turned = pl.BlockSpec((WIDTH, length), lambda g, core: (g, 0))
    summed = pl.BlockSpec((WIDTH, 1), lambda g, core: (g, 0))
    args = (start, cos, sin, na_t, cot) + (weights,) * 3 + (near, far) + (bias_qkv,) * 3
    in_specs = [whole_block(a.shape) for a in args[:5]] + [columns(0), columns(1), columns(2)]
    in_specs += [rows_of_out] * 2 + [entries(0), entries(1), entries(2)]
    out_specs = [whole_block((D, 3 * HALF)), whole_block((HALF, length))]
    out_specs += [turned] * 3 + [summed] * 3
    out_shape = [sd((D, 3 * HALF), bf16)] + [sd((HALF, length), bf16)] * 4
    out_shape += [sd((HALF, 1), f32)] * 3
    return call(
        attention_kernel, (2,), in_specs, out_specs, out_shape, args,
        scratch=[
            pltpu.VMEM((length, length), f32),
            pltpu.VMEM((WIDTH, length), bf16),
            pltpu.VMEM((WIDTH, length), f32),
            pltpu.VMEM((WIDTH, length), f32),
            pltpu.VMEM((WIDTH, length), f32),
            pltpu.VMEM((HEAD_DIM, length), f32),
            pltpu.VMEM((HEAD_DIM, length), f32),
        ],
        flops=50 * 10**9, moved=2 * 10**7,
    )(core, *args)


def ffn_kernel(
    core, nm, cot, w_in, w_down, b_in, merged_near, merged_far, *refs, which
):
    far, near, active_out, grad_out, grad_b = refs[-5:]
    hidden = mul(nm[...], w_in[...], 1, 0) + b_in[...]
    cdf = 0.5 * (1.0 + lax.erf(hidden * (2.0**-0.5)))
    pdf = jnp.exp(-0.5 * hidden * hidden) * (1.0 / math.sqrt(2.0 * math.pi))
    active = (hidden * cdf).astype(bf16)
    grad_hidden = (mul(cot[...], w_down[...], 1, 1) * (cdf + hidden * pdf)).astype(bf16)
    active_out[...], grad_out[...] = active, grad_hidden
    grad_b[...] = jnp.sum(grad_hidden.astype(f32), axis=0, keepdims=True)
    blocks = far.shape[0]
    merged = jnp.where(core[0] == which, merged_near[...], merged_far[...])
    grad_down = mul(active, cot[...], 0, 0).astype(bf16).reshape(blocks, -1, D)
    grad_wo = mul(merged, cot[...], 1, 0).astype(bf16).reshape(blocks, -1, D)
    at, left = grad_down.shape[1], core[0] == 0
    for rows, grad in ((slice(0, at), grad_down), (slice(at, None), grad_wo)):
        far[:, rows, :] = jnp.where(left, grad[..., HALF:], grad[..., :HALF])
        near[:, rows, :] = jnp.where(left, grad[..., :HALF], grad[..., HALF:])


def ffn_first(*refs):
    ffn_kernel(*refs, which=0)


def ffn_second(*refs):
    ffn_kernel(*refs, which=1)


def ffn(core, which, blocks, nm, cot, w_in, w_down, b_in, merged, after, before=()):
    length = nm.shape[0]
    sd = jax.ShapeDtypeStruct
    steps = FF // FF_TILE // 2
    share = (blocks // (2 * steps), (FF + D) // blocks, HALF)
    columns = pl.BlockSpec((D, FF_TILE), lambda g, core: (0, steps * which + g))
    tall = pl.BlockSpec((length, FF_TILE), lambda g, core: (0, steps * which + g))
    row = pl.BlockSpec((1, FF_TILE), lambda g, core: (0, steps * which + g))
    wide = pl.BlockSpec((FF_TILE, D), lambda g, core: (steps * which + g, 0))
    heads = pl.BlockSpec((HALF // steps, length), lambda g, core: (g, 0))
    grads = pl.BlockSpec(share, lambda g, core: (steps * which + g, 0, 0))
    args = (nm, cot, w_in, w_down, b_in) + merged
    more = tuple(before) + tuple(after)
    return call(
        ffn_second if which else ffn_first, (steps,),
        [whole_block((length, D))] * 2 + [columns, wide, row, heads, heads],
        [grads, grads, tall, tall, row],
        [sd((blocks,) + share[1:], bf16)] * 2 + [sd((length, FF), bf16)] * 2 + [sd((1, FF), f32)],
        args, more, aliases={1 + len(args) + at: at for at in range(len(before))},
        flops=16 * 10**9, moved=3 * 10**7,
    )(core, *args, *more)


def grad_in_kernel(core, nm_t, grad_hidden, far, near):
    step = pl.program_id(0)
    half = pl.num_programs(0) // 2

    def store(ref):
        ref[...] = mul(nm_t[...], grad_hidden[...], 1, 0).astype(bf16)

    pl.when(step < half)(lambda: store(far))
    pl.when(step >= half)(lambda: store(near))


def grads_in(core, nm_t, grad_hidden, after):
    length = nm_t.shape[1]
    sd = jax.ShapeDtypeStruct
    half = FF // FF_TILE // 2
    args = (nm_t, grad_hidden)
    return call(
        grad_in_kernel, (2 * half,),
        [
            whole_block((D, length)),
            pl.BlockSpec(
                (length, FF_TILE), lambda g, core: (0, lax.rem(g + (1 - core[0]) * half, 2 * half))
            ),
        ],
        [
            pl.BlockSpec((D, FF_TILE), lambda g, core: (0, jnp.minimum(g, half - 1))),
            pl.BlockSpec((D, FF_TILE), lambda g, core: (0, jnp.maximum(g - half, 0))),
        ],
        [sd((D, FF // 2), bf16)] * 2, args, after, flops=9 * 10**9, moved=2 * 10**7,
    )(core, *args, *after)


def output_kernel(core, tokens, near_t, far_t, active, wo_near, wo_far, w_down, b_sum, output):
    merged_t = by_core(core, near_t[...], far_t[...], 0)
    att = by_core(core, mul(merged_t, wo_near[...], 0, 0), mul(merged_t, wo_far[...], 0, 0), 1)
    fed = mul(active[...], w_down[...], 1, 0)
    output[...] = (tokens[...].astype(f32) + att + fed + b_sum[...]).astype(bf16)


def outputs(core, tokens, near_t, far_t, active, near, far, w_down, b_sum, after):
    length = tokens.shape[0]
    tile = pl.BlockSpec((TOKEN_TILE, D), lambda g, core: (g, 0))
    turned = pl.BlockSpec((HALF, TOKEN_TILE), lambda g, core: (0, g))
    out_columns = pl.BlockSpec((D, HALF), lambda g, core: (0, 3), pipeline_mode=pl.Buffered(1))
    args = (tokens, near_t, far_t, active, near, far, w_down, b_sum)
    return call(
        output_kernel, (length // TOKEN_TILE,),
        [tile, turned, turned, pl.BlockSpec((TOKEN_TILE, FF), lambda g, core: (g, 0))]
        + [out_columns] * 2 + [whole_block((FF, D)), whole_block((1, D))],
        [tile], [jax.ShapeDtypeStruct((length, D), bf16)], args, after,
        flops=11 * 10**9, moved=3 * 10**7,
    )(core, *args, *after)[0]


def input_kernel(
    core, tokens, cot, gq_near, gk_near, gv_near, gq_far, gk_far, gv_far, grad_hidden,
    near, far, w_in, gain_one, gain_two, input_grad, sums,
):
    inputs = tokens[...].astype(f32)
    centre = inputs - jnp.mean(inputs, axis=-1, keepdims=True)
    spread = jnp.mean(centre * centre, axis=-1, keepdims=True)
    rstd = lax.rsqrt(spread + norm_eps)
    normed = centre * rstd
    joined_near = jnp.concatenate([gq_near[...], gk_near[...], gv_near[...]], axis=0)
    joined_far = jnp.concatenate([gq_far[...], gk_far[...], gv_far[...]], axis=0)
    grad_na = mul(joined_near, near[...], 0, 1) + mul(joined_far, far[...], 0, 1)
    grad_nm = mul(grad_hidden[...], w_in[...], 1, 1)
    grad_normed = grad_na * gain_one[...] + grad_nm * gain_two[...]
    cotangent = cot[...].astype(f32)
    input_grad[...] = cotangent + rstd * (
        grad_normed
        - jnp.mean(grad_normed, axis=-1, keepdims=True)
        - normed * jnp.mean(grad_normed * normed, axis=-1, keepdims=True)
    )

    @pl.when(pl.program_id(0) == 0)
    def _():
        sums[...] = jnp.zeros_like(sums)

    for at, terms in enumerate((cotangent, grad_na * normed, grad_na, grad_nm * normed, grad_nm)):
        sums[at : at + 1, :] += jnp.sum(terms, axis=0, keepdims=True)


def input_grads(core, tokens, cot, joined, grad_hidden, near, far, w_in, gains, after):
    length = tokens.shape[0]
    tile = pl.BlockSpec((TOKEN_TILE, D), lambda g, core: (g, 0))
    turned = pl.BlockSpec((HALF, TOKEN_TILE), lambda g, core: (0, g))
    share = pl.BlockSpec((D, 3 * HALF), lambda g, core: (0, 0), pipeline_mode=pl.Buffered(1))
    args = (tokens, cot) + joined + (grad_hidden, near, far, w_in) + gains
    sd = jax.ShapeDtypeStruct
    return call(
        input_kernel, (length // TOKEN_TILE,),
        [tile, tile] + [turned] * 6 + [pl.BlockSpec((TOKEN_TILE, FF), lambda g, core: (g, 0))]
        + [share] * 2 + [whole_block((D, FF))] + [whole_block((1, D))] * 2,
        [tile, whole_block((8, D))],
        [sd((length, D), f32), sd((8, D), f32)], args, after, flops=15 * 10**9, moved=4 * 10**7,
    )(core, *args, *after)


def round_kernel(core, value, low):
    low[...] = value[...].astype(bf16)


def rounded(core, value, after):
    block = whole_block(value.shape)
    low = jax.ShapeDtypeStruct(value.shape, bf16)
    return call(round_kernel, (1,), [block], [block], [low], (value,), after)(core, value, *after)[0]


def later(value, *after):
    return lax.optimization_barrier((value,) + after)[0]


class Links:
    def __init__(self, sizes):
        self.sizes = sizes
        self.nz = sizes["z"]
        self.every = tuple(sizes)

    def swap(self, axis, value, bit=1):
        return lax.ppermute(value, axis, [(i, i ^ bit) for i in range(self.sizes[axis])])

    def bits(self, axis):
        return [1 << i for i in range(self.sizes[axis].bit_length() - 1)]

    def total(self, value):
        for axis in self.every[::-1]:
            for bit in self.bits(axis):
                value = value + self.swap(axis, value, bit)
        return value

    def gather(self, value):
        x, y, z = (lax.axis_index(axis) for axis in "xyz")

        def ordered(at, own, other):
            return jnp.where(
                at == 0, jnp.concatenate([own, other]), jnp.concatenate([other, own])
            )

        column = value[None]
        for bit in self.bits("z")[:-1]:
            column = ordered(z // (2 * bit) % 2, column, self.swap("z", column, 2 * bit))
        other = self.swap("z", column)
        self.column = other
        even = jnp.where(z % 2 == 0, column, other)[:, None, None, None]
        odd = jnp.where(z % 2 == 0, other, column)[:, None, None, None]
        even_y, odd_x = self.swap("y", even), self.swap("x", odd)
        even = jnp.where(
            y == 0, jnp.concatenate([even, even_y], 2), jnp.concatenate([even_y, even], 2)
        )
        odd = jnp.where(
            x == 0, jnp.concatenate([odd, odd_x], 3), jnp.concatenate([odd_x, odd], 3)
        )
        even_x, odd_y = self.swap("x", even), self.swap("y", odd)
        whole = jnp.zeros((self.nz // 2, 2, 2, 2) + value.shape, value.dtype)
        for part, at in (
            (even, (0, 0, x)), (even_x, (0, 0, 1 - x)), (odd, (1, y, 0)), (odd_y, (1, 1 - y, 0))
        ):
            whole = lax.dynamic_update_slice(whole, part, (0,) + at + (0, 0))
        return whole.reshape(-1, value.shape[-1])

    def owners(self, held, core, parts=1):
        cuts = [held.shape[0] * 4 // 5] if parts == 2 else []
        mine, other = [], []
        for part in jnp.split(held, cuts):
            rows = part.shape[0] // 2
            mine.append(lax.dynamic_slice_in_dim(part, core * rows, rows))
            other.append(lax.dynamic_slice_in_dim(part, (1 - core) * rows, rows))
        mine = jnp.concatenate(mine)
        came = self.swap("c", jnp.concatenate(other))
        return jnp.concatenate(
            [jnp.where(core == 0, mine, came), jnp.where(core == 0, came, mine)], axis=1
        )


class Scatter:
    def __init__(self, links, near, came):
        self.links, split = links, (links.nz // 2, 2, 2, 2, -1, near.shape[-1])
        self.near, self.came = near.reshape(split), came.reshape(split)
        self.x, self.y, self.z = (lax.axis_index(axis) for axis in "xyz")
        self.first = (
            self.term(0, x=1 - self.x).astype(bf16),
            self.term(1, y=1 - self.y).astype(bf16),
        )

    def term(self, odd, y=None, x=None):
        def cut(v):
            v = v[:, odd]
            if x is not None:
                v = lax.dynamic_index_in_dim(v, x, 2, False)
            if y is not None:
                v = lax.dynamic_index_in_dim(v, y, 1, False)
            return v.astype(f32)

        return cut(self.near) + cut(self.came)

    def came_at(self, part, at):
        return lax.dynamic_index_in_dim(part, at, 1, False).astype(f32)

    def step_one(self, *after):
        even, odd = self.links.swap("x", self.first[0]), self.links.swap("y", self.first[1])
        self.even, self.odd = later((even, odd), *after)
        x, y = self.x, self.y
        self.second = (
            (self.term(0, 1 - y, x) + self.came_at(self.even, 1 - y)).astype(bf16),
            (self.term(1, y, 1 - x) + self.came_at(self.odd, 1 - x)).astype(bf16),
        )

    def step_two(self, *after):
        even, odd = self.links.swap("y", self.second[0]), self.links.swap("x", self.second[1])
        even, odd = later((even, odd), *after)
        x, y = self.x, self.y
        even = self.term(0, y, x) + self.came_at(self.even, y) + even.astype(f32)
        odd = self.term(1, y, x) + self.came_at(self.odd, x) + odd.astype(f32)
        low = self.z % 2 == 0
        self.keep, self.send = jnp.where(low, even, odd), jnp.where(low, odd, even).astype(bf16)

    def finish(self, *after):
        came = later(self.links.swap("z", self.send), *after) if after else self.links.swap("z", self.send)
        held = self.keep + came.astype(f32)
        for bit in self.links.bits("z")[:-1][::-1]:
            mine = self.z // (2 * bit) % 2
            send = lax.dynamic_slice_in_dim(held, (1 - mine) * bit, bit).astype(bf16)
            keep = lax.dynamic_slice_in_dim(held, mine * bit, bit)
            held = keep + self.links.swap("z", send, 2 * bit).astype(f32)
        return held[0]


def per_device(
    links,
    tokens,
    cotangent,
    doc_ids,
    w_qkv,
    w_out,
    w_in,
    w_down,
    vectors,
    first_qkv,
    first_out,
    first_in,
    first_down,
    first_vectors,
    second_qkv,
    second_out,
    second_in,
    second_down,
    second_vectors,
):
    every = links.every
    core = lax.axis_index("c")
    core_ref = core.astype(jnp.int32).reshape(1)
    length = tokens.shape[0]
    rows = w_qkv.shape[0]
    per_row = vectors.shape[0] // rows

    spare = jnp.pad(vectors.astype(bf16).reshape(rows, per_row), ((0, 0), (0, 128 - per_row)))
    halves = jnp.concatenate([w_qkv, w_out], axis=1).astype(bf16).reshape(rows, 4, 2, HALF)

    def share(at):
        part = lax.dynamic_index_in_dim(halves, at, 2, False).reshape(rows, 4 * HALF)
        return jnp.concatenate([part, spare], axis=1)

    mine, came = share(core), links.swap("c", share(1 - core))
    near = links.gather(
        jnp.where(core == 0, jnp.concatenate([mine, came]), jnp.concatenate([came, mine]))
    )
    far = links.swap("c", near)
    w_in_all = lax.all_gather(rounded(core_ref, w_in, (links.column,)), every, axis=0, tiled=True)
    w_down_all = lax.all_gather(rounded(core_ref, w_down, (links.column,)), every, axis=0, tiled=True)
    vector_all = near[:, 4 * HALF : 4 * HALF + per_row].reshape(-1).astype(f32)
    b_qkv, b_out, b_in, b_down, gain_one, shift_one, gain_two, shift_two = split_vector(vector_all)

    positions = positions_of(doc_ids)
    start = (jnp.arange(length, dtype=jnp.int32) - positions).reshape(1, length)
    freqs = jnp.exp(jnp.arange(ROT // 2, dtype=f32) * (-2.0 * math.log(10000.0) / ROT))
    angles = freqs[:, None] * positions.astype(f32)[None, :]
    gains = (gain_one.reshape(1, D), gain_two.reshape(1, D))
    na, nm, na_t, nm_t = norms(
        core_ref, tokens, (gains[0], shift_one.reshape(1, D), gains[1], shift_two.reshape(1, D))
    )
    common = (start, jnp.cos(angles), jnp.sin(angles), na_t, cotangent)
    bias_qkv = b_qkv.reshape(3 * D, 1)
    grads_far, merged_far, *joined_far = attention(
        core_ref, False, *common, far, near, far, bias_qkv
    )
    came_heads = links.swap("c", grads_far)
    grads_near, merged_near, *joined_near = attention(
        core_ref, True, *common, near, near, far, bias_qkv
    )
    heads = Scatter(links, grads_near, came_heads)
    blocks = D // rows // 2
    fixed = (nm, cotangent, w_in_all, w_down_all, b_in.reshape(1, FF), (merged_near, merged_far))
    filled = ffn(core_ref, 0, blocks, *fixed, heads.first)
    heads.step_one(filled[4])
    down_far, down_near, active, grad_hidden, sum_in = ffn(
        core_ref, 1, blocks, *fixed, heads.second, filled
    )
    came_down = links.swap("c", down_far)
    heads.step_two(sum_in)
    in_far, in_near = grads_in(core_ref, nm_t, grad_hidden, (heads.send,))
    came_in = links.swap("c", in_far)
    down = Scatter(links, down_near, came_down)
    output = outputs(
        core_ref, tokens, merged_near, merged_far, active, near, far, w_down_all,
        (b_out + b_down).reshape(1, D), down.first,
    )
    grad_heads = links.owners(heads.finish(output[:8, :128]), core)
    inner = Scatter(links, in_near, came_in)
    down.step_one(output[:8, :128])
    input_grad, sums = input_grads(
        core_ref, tokens, cotangent, tuple(joined_near[:3] + joined_far[:3]), grad_hidden,
        near, far, w_in_all, gains, down.second + inner.first + (output,),
    )
    heads_sums = [
        part[:, 0]
        for mine, other in zip(joined_near[3:], joined_far[3:])
        for part in (jnp.where(core == 0, mine, other), jnp.where(core == 0, other, mine))
    ]
    vector_terms = jnp.concatenate(
        heads_sums + [sums[0], sum_in[0], sums[0], sums[1], sums[2], sums[3], sums[4]]
    )
    vector_total = links.total(vector_terms.reshape(-1, 128)).reshape(-1)
    count_own = vectors.shape[0]
    grad_vectors = lax.dynamic_slice_in_dim(
        vector_total, lax.axis_index(every) * count_own, count_own
    )
    grad_qkv = grad_heads.reshape(rows, 2, 3, HALF).transpose(0, 2, 1, 3).reshape(rows, 3 * D)
    down.step_two(sums)
    inner.step_one(sums)
    grad_rows = links.owners(down.finish(), core, 2)
    grad_down, grad_out = grad_rows[: 4 * rows], grad_rows[4 * rows :]
    inner.step_two()
    grad_in = links.owners(inner.finish(), core)
    pieces = (grad_qkv, grad_out, grad_in, grad_down, grad_vectors)
    local_square = sum(jnp.sum(piece * piece) for piece in pieces)
    norm = jnp.sqrt(links.total(jnp.broadcast_to(local_square, (8, 128)))[0, 0])
    clip = jnp.minimum(1.0, clip_limit / (norm + 1e-06))
    masters = (w_qkv, w_out, w_in, w_down, vectors)
    firsts = (first_qkv, first_out, first_in, first_down, first_vectors)
    seconds = (second_qkv, second_out, second_in, second_down, second_vectors)
    results = [
        adam_step(w, g, f, s, clip, float(STEPS))
        for w, g, f, s in zip(masters, pieces, firsts, seconds)
    ]
    return (output, input_grad, norm.reshape(1)) + pieces + tuple(
        result[at] for at in range(3) for result in results
    )


def solution(mesh):
    fsdp, rep = mesh.shape["fsdp"], mesh.shape["rep"]
    sizes = {"z": fsdp // 2, "y": 2, "x": rep // 2, "c": 2}
    cut = Mesh(mesh.devices.reshape(tuple(sizes.values())), tuple(sizes))
    names = tuple(sizes)
    wide, flat = P(names, None), P(names)
    group = (wide, wide, wide, wide, flat)
    body = jax.shard_map(
        functools.partial(per_device, Links(sizes)),
        mesh=cut,
        in_specs=(wide, wide, flat) + group * 3,
        out_specs=(wide, wide, P()) + group * 4,
        check_vma=False,
    )
    return body
```

```python
import functools
import math

import jax
import jax.numpy as jnp
from jax import lax
from jax.experimental import pallas as pl
from jax.experimental.pallas import tpu as pltpu
from jax.sharding import Mesh
from jax.sharding import PartitionSpec as P

D = 1024
FF = 4096
HEAD_DIM = 64
ROT = 16
STEPS = 10

first_decay = 0.9
second_decay = 0.95
adam_eps = 1e-08
weight_decay = 0.1
learn_rate = 0.02
clip_limit = 1.0
norm_eps = 1e-05

bf16 = jnp.bfloat16
f32 = jnp.float32

HEADS_STEP = 4
WIDTH = HEADS_STEP * HEAD_DIM
QUERY_ROWS = 256
FF_TILE = 512
TOKEN_TILE = 256
HALF = D // 2
VMEM_BYTES = 58 * 2**20


def mul(a, b, dim_a, dim_b):
    return lax.dot_general(a, b, (((dim_a,), (dim_b,)), ((), ())), preferred_element_type=f32)


def positions_of(segments):
    index = jnp.arange(segments.shape[0], dtype=jnp.int32)
    starts = jnp.concatenate([jnp.ones((1,), dtype=bool), segments[1:] != segments[:-1]])
    first = lax.cummax(jnp.where(starts, index, jnp.zeros_like(index)), axis=0)
    return index - first


def split_vector(vector):
    cuts = [3 * D, 4 * D, 4 * D + FF, 5 * D + FF, 6 * D + FF, 7 * D + FF, 8 * D + FF]
    return jnp.split(vector, cuts)


def adam_step(weight, grad, first, second, clip, count):
    scaled = grad * clip
    new_first = first_decay * first + (1.0 - first_decay) * scaled
    new_second = second_decay * second + (1.0 - second_decay) * scaled * scaled
    fix_one = 1.0 - first_decay**count
    fix_two = 1.0 - second_decay**count
    change = -learn_rate * (
        new_first / fix_one / (jnp.sqrt(new_second / fix_two) + adam_eps) + weight_decay * weight
    )
    return (new_first, new_second, change)


def call(kernel, grid, in_specs, out_specs, out_shape, args, after=(), scratch=(), aliases=None, flops=0, moved=0):
    count = len(args)

    def run(*refs):
        kernel(*refs[: 1 + count], *refs[1 + count + len(after) :])

    return pl.pallas_call(
        run,
        grid_spec=pltpu.PrefetchScalarGridSpec(
            num_scalar_prefetch=1,
            grid=grid,
            in_specs=list(in_specs) + [pl.BlockSpec(memory_space=pl.ANY)] * len(after),
            out_specs=list(out_specs),
            scratch_shapes=list(scratch),
        ),
        out_shape=list(out_shape),
        input_output_aliases=aliases or {},
        compiler_params=pltpu.CompilerParams(vmem_limit_bytes=VMEM_BYTES),
        cost_estimate=pl.CostEstimate(flops=flops, bytes_accessed=moved, transcendentals=0),
        name=kernel.__name__,
    )


def whole_block(shape):
    return pl.BlockSpec(shape, lambda g, core: (0,) * len(shape), pipeline_mode=pl.Buffered(1))


def by_core(core, near, far, axis):
    return jnp.where(
        core[0] == 0,
        jnp.concatenate([near, far], axis=axis),
        jnp.concatenate([far, near], axis=axis),
    )


def norm_kernel(core, tokens, gain_one, shift_one, gain_two, shift_two, na, nm, na_t, nm_t):
    inputs = tokens[...].astype(f32)
    centre = inputs - jnp.mean(inputs, axis=-1, keepdims=True)
    spread = jnp.mean(centre * centre, axis=-1, keepdims=True)
    normed = centre * lax.rsqrt(spread + norm_eps)
    one = (normed * gain_one[...] + shift_one[...]).astype(bf16)
    two = (normed * gain_two[...] + shift_two[...]).astype(bf16)
    na[...], nm[...], na_t[...], nm_t[...] = one, two, one.T, two.T


def norms(core, tokens, rows):
    length = tokens.shape[0]
    tile = pl.BlockSpec((TOKEN_TILE, D), lambda g, core: (g, 0))
    turned = pl.BlockSpec((D, TOKEN_TILE), lambda g, core: (0, g))
    sd = jax.ShapeDtypeStruct
    return call(
        norm_kernel, (length // TOKEN_TILE,), [tile] + [whole_block((1, D))] * 4,
        [tile, tile, turned, turned],
        [sd((length, D), bf16)] * 2 + [sd((D, length), bf16)] * 2,
        (tokens,) + rows, flops=10**7, moved=10**7,
    )(core, tokens, *rows)


def attention_kernel(core, start, cos, sin, na_t, cot, wq, wk, wv, wo, bq, bk, bv, *refs):
    refs, scratch = refs[:-7], refs[-7:]
    grads, merged, gq_out, gk_out, gv_out, sum_q, sum_k, sum_v = refs[-8:]
    bias, merged_t, gq_t, gk_t, gv_t, acc_k, acc_v = scratch
    length = cot.shape[0]

    @pl.when(pl.program_id(0) == 0)
    def _():
        key = lax.broadcasted_iota(jnp.int32, (length, length), 0)
        query = lax.broadcasted_iota(jnp.int32, (length, length), 1)
        bias[...] = jnp.where((key >= start[...]) & (key <= query), 0.0, -1e30)

    c, s = cos[...], sin[...]

    def project(w, b):
        return mul(w[...], na_t[...], 0, 0) + b[...]

    def rotate(v, sign):
        rows = []
        for h in range(HEADS_STEP):
            at = h * HEAD_DIM
            lo, hi = v[at : at + 8], v[at + 8 : at + 16]
            rows += [lo * c - sign * (hi * s), hi * c + sign * (lo * s), v[at + 16 : at + HEAD_DIM]]
        return jnp.concatenate(rows, axis=0)

    scale = HEAD_DIM**-0.5
    q_t = rotate(project(wq, bq), 1.0).astype(bf16) * jnp.asarray(scale, bf16)
    k_t = rotate(project(wk, bk), 1.0).astype(bf16)
    v_t = project(wv, bv).astype(bf16)
    gm_t = mul(wo[...], cot[...], 1, 1).astype(bf16)
    k, v = k_t.T, v_t.T
    for h in range(HEADS_STEP):
        hs = slice(h * HEAD_DIM, (h + 1) * HEAD_DIM)
        acc_k[...] = jnp.zeros_like(acc_k)
        acc_v[...] = jnp.zeros_like(acc_v)
        for i in range(length // QUERY_ROWS):
            n = QUERY_ROWS * (i + 1)
            qs = slice(i * QUERY_ROWS, n)
            scores = mul(k[:n, hs], q_t[hs, qs], 1, 0) + bias[:n, qs]
            weights = jnp.exp(scores - jnp.max(scores, axis=0, keepdims=True))
            probs = weights * (1.0 / jnp.sum(weights, axis=0, keepdims=True))
            probs_low = probs.astype(bf16)
            merged_t[hs, qs] = mul(v_t[hs, :n], probs_low, 1, 0).astype(bf16)
            grad_probs = mul(v[:n, hs], gm_t[hs, qs], 1, 0)
            inner = jnp.sum(grad_probs * probs, axis=0, keepdims=True)
            grad_scores = (probs * (grad_probs - inner)).astype(bf16)
            gq_t[hs, qs] = mul(k_t[hs, :n], grad_scores, 1, 0) * scale
            acc_k[:, :n] += mul(q_t[hs, qs], grad_scores, 1, 1)
            acc_v[:, :n] += mul(gm_t[hs, qs], probs_low, 1, 1)
        gk_t[hs, :] = acc_k[...]
        gv_t[hs, :] = acc_v[...]
    gq = rotate(gq_t[...], -1.0).astype(bf16)
    gk = rotate(gk_t[...], -1.0).astype(bf16)
    gv = gv_t[...].astype(bf16)
    merged[...], gq_out[...], gk_out[...], gv_out[...] = merged_t[...], gq, gk, gv
    for at, (part, out) in enumerate(((gq, sum_q), (gk, sum_k), (gv, sum_v))):
        out[...] = jnp.sum(part.astype(f32), axis=1, keepdims=True)
        grads[:, at * WIDTH : (at + 1) * WIDTH] = mul(na_t[...], part, 1, 1).astype(bf16)


def attention(core, own, part, parts, start, cos, sin, na_t, cot, weights, bias_qkv, before=(), grads=None):
    length = cot.shape[0]

    def at(core, g):
        return part + g + 2 * (core[0] if own else 1 - core[0])

    def columns(kind):
        return pl.BlockSpec((D, WIDTH), lambda g, core: (0, 4 * kind + at(core, g)))

    def entries(kind):
        return pl.BlockSpec((WIDTH, 1), lambda g, core: (4 * kind + at(core, g), 0))

    sd = jax.ShapeDtypeStruct
    args = (start, cos, sin, na_t, cot) + (weights,) * 4 + (bias_qkv,) * 3
    in_specs = [whole_block(a.shape) for a in args[:5]] + [columns(0), columns(1), columns(2)]
    in_specs += [pl.BlockSpec((WIDTH, D), lambda g, core: (at(core, g), 3))]
    in_specs += [entries(0), entries(1), entries(2)]
    out_specs = [pl.BlockSpec((D, 3 * WIDTH), lambda g, core: (0, part + g))]
    out_specs += [pl.BlockSpec((WIDTH, length), lambda g, core: (at(core, g), 0))] * 4
    out_specs += [entries(0)] * 3
    out_shape = [sd((D, 4 * HALF), bf16)] + [sd((D, length), bf16)] * 4 + [sd((D, 1), f32)] * 3
    kept = ((grads,) if grads is not None else ()) + tuple(before)
    first = 1 + len(args)
    return call(
        attention_kernel, (parts,), in_specs, out_specs, out_shape, args, kept,
        aliases={first + i: len(out_shape) - len(kept) + i for i in range(len(kept))},
        scratch=[
            pltpu.VMEM((length, length), f32),
            pltpu.VMEM((WIDTH, length), bf16),
            pltpu.VMEM((WIDTH, length), f32),
            pltpu.VMEM((WIDTH, length), f32),
            pltpu.VMEM((WIDTH, length), f32),
            pltpu.VMEM((HEAD_DIM, length), f32),
            pltpu.VMEM((HEAD_DIM, length), f32),
        ],
        flops=parts * 25 * 10**9, moved=2 * 10**7,
    )(core, *args, *kept)


def grad_out_kernel(core, merged, cot, far, near):
    grad = mul(merged[...], cot[...], 1, 0).astype(bf16)
    left = core[0] == 0
    far[...] = jnp.where(left, grad[:, HALF:], grad[:, :HALF])
    near[...] = jnp.where(left, grad[:, :HALF], grad[:, HALF:])


def grads_out(core, merged, cot, near):
    args = (merged, cot)
    rows = pl.BlockSpec((WIDTH, cot.shape[0]), lambda g, core: (g, 0))
    return call(
        grad_out_kernel, (D // WIDTH,), [rows, whole_block(cot.shape)],
        [
            pl.BlockSpec((WIDTH, HALF), lambda g, core: (g, 0)),
            pl.BlockSpec((WIDTH, HALF), lambda g, core: (g, 3)),
        ],
        [jax.ShapeDtypeStruct((D, HALF), bf16), jax.ShapeDtypeStruct(near.shape, bf16)],
        args, (near,), aliases={1 + len(args): 1}, flops=3 * 10**9, moved=10**7,
    )(core, *args, near)


def ffn_kernel(
    core, nm, cot, w_in, wd_near, wd_far, b_in, far, near, active_out, grad_out, grad_b
):
    w_down = by_core(core, wd_near[...], wd_far[...], 1)
    hidden = mul(nm[...], w_in[...], 1, 0) + b_in[...]
    cdf = 0.5 * (1.0 + lax.erf(hidden * (2.0**-0.5)))
    pdf = jnp.exp(-0.5 * hidden * hidden) * (1.0 / math.sqrt(2.0 * math.pi))
    active = (hidden * cdf).astype(bf16)
    grad_hidden = (mul(cot[...], w_down, 1, 1) * (cdf + hidden * pdf)).astype(bf16)
    active_out[...], grad_out[...] = active, grad_hidden
    grad_b[...] = jnp.sum(grad_hidden.astype(f32), axis=0, keepdims=True)
    grad_down = mul(active, cot[...], 0, 0).astype(bf16)
    left = core[0] == 0
    far[...] = jnp.where(left, grad_down[:, HALF:], grad_down[:, :HALF]).reshape(far.shape)
    near[...] = jnp.where(left, grad_down[:, :HALF], grad_down[:, HALF:]).reshape(near.shape)


def ffn(core, blocks, nm, cot, w_in, wd_near, wd_far, b_in):
    length = nm.shape[0]
    deep = FF // blocks
    share = pl.BlockSpec((FF_TILE // deep, deep, HALF), lambda g, core: (g, 0, 0))
    sd = jax.ShapeDtypeStruct
    columns = pl.BlockSpec((D, FF_TILE), lambda g, core: (0, g))
    tall = pl.BlockSpec((length, FF_TILE), lambda g, core: (0, g))
    row = pl.BlockSpec((1, FF_TILE), lambda g, core: (0, g))
    half = pl.BlockSpec((FF_TILE, HALF), lambda g, core: (g, 0))
    args = (nm, cot, w_in, wd_near, wd_far, b_in)
    return call(
        ffn_kernel, (FF // FF_TILE,),
        [whole_block((length, D))] * 2 + [columns, half, half, row],
        [share, share, tall, tall, row],
        [sd((blocks, 2 * deep, HALF), bf16)] * 2 + [sd((length, FF), bf16)] * 2 + [sd((1, FF), f32)],
        args, flops=30 * 10**9, moved=5 * 10**7,
    )(core, *args)


def grad_in_kernel(core, nm_t, grad_hidden, far, near):
    step = pl.program_id(0)
    half = pl.num_programs(0) // 2

    def store(ref):
        ref[...] = mul(nm_t[...], grad_hidden[...], 1, 0).astype(bf16).reshape(ref.shape)

    pl.when(step < half)(lambda: store(far))
    pl.when(step >= half)(lambda: store(near))


def grads_in(core, nm_t, grad_hidden, far, near):
    length = nm_t.shape[1]
    blocks = far.shape[0]
    half = FF // FF_TILE // 2
    split = (blocks, 2 * half, D // blocks, FF_TILE)
    args = (nm_t, grad_hidden)
    first = 1 + len(args)
    cut = (blocks, 1, D // blocks, FF_TILE)
    return call(
        grad_in_kernel, (2 * half,),
        [
            whole_block((D, length)),
            pl.BlockSpec(
                (length, FF_TILE), lambda g, core: (0, lax.rem(g + (1 - core[0]) * half, 2 * half))
            ),
        ],
        [
            pl.BlockSpec(cut, lambda g, core: (0, half + jnp.minimum(g, half - 1), 0, 0)),
            pl.BlockSpec(cut, lambda g, core: (0, half + jnp.maximum(g - half, 0), 0, 0)),
        ],
        [jax.ShapeDtypeStruct(split, bf16)] * 2, args, (far.reshape(split), near.reshape(split)),
        aliases={first: 0, first + 1: 1}, flops=9 * 10**9, moved=2 * 10**7,
    )(core, *args, far.reshape(split), near.reshape(split))


def output_kernel(core, tokens, merged, active, wo, wd_near, wd_far, b_sum, output):
    att = mul(merged[...], wo[...], 0, 0)
    fed = by_core(
        core, mul(active[...], wd_near[...], 1, 0), mul(active[...], wd_far[...], 1, 0), 1
    )
    output[...] = (tokens[...].astype(f32) + att + fed + b_sum[...]).astype(bf16)


def outputs(core, tokens, merged, active, weights, wd_near, wd_far, b_sum, after):
    length = tokens.shape[0]
    tile = pl.BlockSpec((TOKEN_TILE, D), lambda g, core: (g, 0))
    turned = pl.BlockSpec((D, TOKEN_TILE), lambda g, core: (0, g))
    w_out = pl.BlockSpec((D, D), lambda g, core: (0, 3), pipeline_mode=pl.Buffered(1))
    args = (tokens, merged, active, weights, wd_near, wd_far, b_sum)
    return call(
        output_kernel, (length // TOKEN_TILE,),
        [tile, turned, pl.BlockSpec((TOKEN_TILE, FF), lambda g, core: (g, 0)), w_out]
        + [whole_block((FF, HALF))] * 2 + [whole_block((1, D))],
        [tile], [jax.ShapeDtypeStruct((length, D), bf16)], args, after,
        flops=11 * 10**9, moved=3 * 10**7,
    )(core, *args, *after)[0]


def input_kernel(
    core, tokens, cot, gq, gk, gv, grad_hidden, w_qkv, w_in, gain_one, gain_two, input_grad, sums
):
    inputs = tokens[...].astype(f32)
    centre = inputs - jnp.mean(inputs, axis=-1, keepdims=True)
    spread = jnp.mean(centre * centre, axis=-1, keepdims=True)
    rstd = lax.rsqrt(spread + norm_eps)
    normed = centre * rstd
    joined = jnp.concatenate([gq[...], gk[...], gv[...]], axis=0)
    grad_na = mul(joined, w_qkv[...], 0, 1)
    grad_nm = mul(grad_hidden[...], w_in[...], 1, 1)
    grad_normed = grad_na * gain_one[...] + grad_nm * gain_two[...]
    cotangent = cot[...].astype(f32)
    input_grad[...] = cotangent + rstd * (
        grad_normed
        - jnp.mean(grad_normed, axis=-1, keepdims=True)
        - normed * jnp.mean(grad_normed * normed, axis=-1, keepdims=True)
    )

    @pl.when(pl.program_id(0) == 0)
    def _():
        sums[...] = jnp.zeros_like(sums)

    for at, terms in enumerate((cotangent, grad_na * normed, grad_na, grad_nm * normed, grad_nm)):
        sums[at : at + 1, :] += jnp.sum(terms, axis=0, keepdims=True)


def input_grads(core, tokens, cot, joined, grad_hidden, weights, w_in, gains, after):
    length = tokens.shape[0]
    tile = pl.BlockSpec((TOKEN_TILE, D), lambda g, core: (g, 0))
    turned = pl.BlockSpec((D, TOKEN_TILE), lambda g, core: (0, g))
    once = functools.partial(pl.BlockSpec, pipeline_mode=pl.Buffered(1))
    args = (tokens, cot) + joined + (grad_hidden, weights, w_in) + gains
    sd = jax.ShapeDtypeStruct
    return call(
        input_kernel, (length // TOKEN_TILE,),
        [tile, tile] + [turned] * 3 + [pl.BlockSpec((TOKEN_TILE, FF), lambda g, core: (g, 0))]
        + [once((D, 3 * D), lambda g, core: (0, 0)), once((D, FF), lambda g, core: (0, 0))]
        + [whole_block((1, D))] * 2,
        [tile, whole_block((8, D))],
        [sd((length, D), f32), sd((8, D), f32)], args, after, flops=15 * 10**9, moved=4 * 10**7,
    )(core, *args, *after)


def round_kernel(core, value, low):
    low[...] = value[...].astype(bf16)


def rounded(core, value, after):
    block = whole_block(value.shape)
    low = jax.ShapeDtypeStruct(value.shape, bf16)
    return call(round_kernel, (1,), [block], [block], [low], (value,), after)(core, value, *after)[0]


def later(value, *after):
    return lax.optimization_barrier((value,) + after)[0]


class Links:
    def __init__(self, sizes):
        self.sizes = sizes
        self.nz = sizes["z"]
        self.every = tuple(sizes)

    def swap(self, axis, value, bit=1):
        return lax.ppermute(value, axis, [(i, i ^ bit) for i in range(self.sizes[axis])])

    def bits(self, axis):
        return [1 << i for i in range(self.sizes[axis].bit_length() - 1)]

    def total(self, value):
        for axis in self.every[::-1]:
            for bit in self.bits(axis):
                value = value + self.swap(axis, value, bit)
        return value

    def gather(self, value):
        x, y, z = (lax.axis_index(axis) for axis in "xyz")

        def ordered(at, own, other):
            return jnp.where(
                at == 0, jnp.concatenate([own, other]), jnp.concatenate([other, own])
            )

        column = value[None]
        for bit in self.bits("z")[:-1]:
            column = ordered(z // (2 * bit) % 2, column, self.swap("z", column, 2 * bit))
        other = self.swap("z", column)
        self.column = other
        even = jnp.where(z % 2 == 0, column, other)[:, None, None, None]
        odd = jnp.where(z % 2 == 0, other, column)[:, None, None, None]
        even_y, odd_x = self.swap("y", even), self.swap("x", odd)
        even = jnp.where(
            y == 0, jnp.concatenate([even, even_y], 2), jnp.concatenate([even_y, even], 2)
        )
        odd = jnp.where(
            x == 0, jnp.concatenate([odd, odd_x], 3), jnp.concatenate([odd_x, odd], 3)
        )
        even_x, odd_y = self.swap("x", even), self.swap("y", odd)
        whole = jnp.zeros((self.nz // 2, 2, 2, 2) + value.shape, value.dtype)
        for part, at in (
            (even, (0, 0, x)), (even_x, (0, 0, 1 - x)), (odd, (1, y, 0)), (odd_y, (1, 1 - y, 0))
        ):
            whole = lax.dynamic_update_slice(whole, part, (0,) + at + (0, 0))
        return whole.reshape(-1, value.shape[-1])

    def owners(self, held, core):
        rows = held.shape[0] // 2
        mine = lax.dynamic_slice_in_dim(held, core * rows, rows)
        came = self.swap("c", lax.dynamic_slice_in_dim(held, (1 - core) * rows, rows))
        return jnp.concatenate(
            [jnp.where(core == 0, mine, came), jnp.where(core == 0, came, mine)], axis=1
        )


class Scatter:
    def __init__(self, links, near, came):
        self.links, split = links, (links.nz // 2, 2, 2, 2, -1, near.shape[-1])
        self.near, self.came = near.reshape(split), came.reshape(split)
        self.x, self.y, self.z = (lax.axis_index(axis) for axis in "xyz")
        self.first = (
            self.term(0, x=1 - self.x).astype(bf16),
            self.term(1, y=1 - self.y).astype(bf16),
        )

    def term(self, odd, y=None, x=None):
        _, _, _, _, rows, n = self.near.shape
        size = (self.links.nz // 2, 1, 1 if y is not None else 2, 1 if x is not None else 2, rows, n)
        start = (0, odd, 0 if y is None else y, 0 if x is None else x, 0, 0)
        shape = tuple(count for at, count in enumerate(size) if at in (0, 4, 5) or count == 2)

        def cut(v):
            return lax.dynamic_slice(v, start, size).reshape(shape).astype(f32)

        return cut(self.near) + cut(self.came)

    def came_at(self, part, at):
        return lax.dynamic_index_in_dim(part, at, 1, False).astype(f32)

    def step_one(self, *after):
        even, odd = self.links.swap("x", self.first[0]), self.links.swap("y", self.first[1])
        self.even, self.odd = later((even, odd), *after)
        x, y = self.x, self.y
        self.second = (
            (self.term(0, 1 - y, x) + self.came_at(self.even, 1 - y)).astype(bf16),
            (self.term(1, y, 1 - x) + self.came_at(self.odd, 1 - x)).astype(bf16),
        )

    def step_two(self, *after):
        even, odd = self.links.swap("y", self.second[0]), self.links.swap("x", self.second[1])
        even, odd = later((even, odd), *after)
        x, y = self.x, self.y
        even = self.term(0, y, x) + self.came_at(self.even, y) + even.astype(f32)
        odd = self.term(1, y, x) + self.came_at(self.odd, x) + odd.astype(f32)
        low = self.z % 2 == 0
        self.keep, self.send = jnp.where(low, even, odd), jnp.where(low, odd, even).astype(bf16)

        self.bits = [1] + [2 * bit for bit in self.links.bits("z")[:-1]][::-1]

    def advance(self, *after):
        came = self.links.swap("z", self.send, self.bits.pop(0))
        self.held = self.keep + (later(came, *after) if after else came).astype(f32)
        if self.bits:
            bit = self.bits[0]
            mine, size = self.z // bit % 2, bit // 2
            self.send = lax.dynamic_slice_in_dim(self.held, (1 - mine) * size, size).astype(bf16)
            self.keep = lax.dynamic_slice_in_dim(self.held, mine * size, size)

    def finish(self):
        while self.bits:
            self.advance()
        return self.held[0]


def per_device(
    links,
    tokens,
    cotangent,
    doc_ids,
    w_qkv,
    w_out,
    w_in,
    w_down,
    vectors,
    first_qkv,
    first_out,
    first_in,
    first_down,
    first_vectors,
    second_qkv,
    second_out,
    second_in,
    second_down,
    second_vectors,
):
    every = links.every
    core = lax.axis_index("c")
    core_ref = core.astype(jnp.int32).reshape(1)
    length = tokens.shape[0]
    rows = w_qkv.shape[0]
    per_row = vectors.shape[0] // rows

    spare = jnp.pad(vectors.reshape(rows, per_row), ((0, 0), (0, 128 - per_row)))
    w_in_all = lax.all_gather(
        jnp.concatenate([w_in, spare], axis=1).astype(bf16), every, axis=0, tiled=True
    )
    halves = w_down.astype(bf16).reshape(-1, 2, HALF)
    mine = lax.dynamic_index_in_dim(halves, core, 1, False)
    came = links.swap("c", lax.dynamic_index_in_dim(halves, 1 - core, 1, False))
    wd_near = links.gather(
        jnp.where(core == 0, jnp.concatenate([mine, came]), jnp.concatenate([came, mine]))
    )
    wd_far = links.swap("c", wd_near)
    weights = lax.all_gather(
        rounded(core_ref, jnp.concatenate([w_qkv, w_out], axis=1), (links.column,)),
        every, axis=0, tiled=True,
    )
    vector_all = w_in_all[:, FF : FF + per_row].reshape(-1).astype(f32)
    b_qkv, b_out, b_in, b_down, gain_one, shift_one, gain_two, shift_two = split_vector(vector_all)

    positions = positions_of(doc_ids)
    start = (jnp.arange(length, dtype=jnp.int32) - positions).reshape(1, length)
    freqs = jnp.exp(jnp.arange(ROT // 2, dtype=f32) * (-2.0 * math.log(10000.0) / ROT))
    angles = freqs[:, None] * positions.astype(f32)[None, :]
    gains = (gain_one.reshape(1, D), gain_two.reshape(1, D))
    na, nm, na_t, nm_t = norms(
        core_ref, tokens, (gains[0], shift_one.reshape(1, D), gains[1], shift_two.reshape(1, D))
    )
    cos, sin = jnp.cos(angles), jnp.sin(angles)
    bias_qkv = b_qkv.reshape(3 * D, 1)
    blocks = D // rows // 2
    far, near, active, grad_hidden, sum_in = ffn(
        core_ref, blocks, nm, cotangent, w_in_all, wd_near, wd_far, b_in.reshape(1, FF)
    )
    far, near = grads_in(core_ref, nm_t, grad_hidden, far, near)
    deep = 2 * FF // blocks
    hidden = Scatter(
        links, near.reshape(blocks * deep, HALF), links.swap("c", far).reshape(blocks * deep, HALF)
    )
    heads = functools.partial(attention, core_ref)

    def common(*after):
        return (later(start, *after), cos, sin, na_t, cotangent, weights, bias_qkv)

    far, *kept = heads(False, 0, 2, *common(*hidden.first))
    came_heads = links.swap("c", far)
    hidden.step_one(kept[4])
    near, *kept = heads(True, 0, 1, *common(*hidden.second), kept)
    hidden.step_two(kept[4])
    near, *kept = heads(True, 1, 1, *common(hidden.send), kept, near)
    merged, *joined = kept[:4]
    hidden.advance(kept[4])
    out_far, near = grads_out(core_ref, merged, later(cotangent, hidden.send), near)
    came_out = links.swap("c", out_far)
    last = Scatter(
        links, near, lax.dynamic_update_slice(came_heads, came_out, (0, 3 * HALF))
    )
    output = outputs(
        core_ref, later(tokens, *last.first, hidden.send), merged, active, weights, wd_near, wd_far,
        (b_out + b_down).reshape(1, D), (),
    )
    last.step_one(output)
    input_grad, sums = input_grads(
        core_ref, later(tokens, *last.second), cotangent, tuple(joined), grad_hidden, weights, w_in_all,
        gains, (output,),
    )
    hidden.advance(output)
    held = hidden.finish()
    deep = deep // 2
    held = jnp.concatenate(
        [
            held[:deep].reshape(2, deep // 2, HALF),
            held[deep:].reshape(-1, 2, rows, HALF).transpose(1, 0, 2, 3).reshape(2, -1, HALF),
        ],
        axis=1,
    ).reshape(-1, HALF)
    grad_rows = links.owners(held, core)
    grad_down = grad_rows[: deep // 2]
    grad_in = grad_rows[deep // 2 :].reshape(-1, rows, 2, HALF).transpose(1, 2, 0, 3).reshape(rows, FF)
    last.step_two(sums)
    vector_terms = jnp.concatenate(
        [part[:, 0] for part in kept[4:]] + [sums[0], sum_in[0], sums[0], sums[1], sums[2], sums[3], sums[4]]
    )
    vector_total = links.total(vector_terms.reshape(-1, 128)).reshape(-1)
    count_own = vectors.shape[0]
    grad_vectors = lax.dynamic_slice_in_dim(
        vector_total, lax.axis_index(every) * count_own, count_own
    )
    grad_heads = links.owners(last.finish(), core).reshape(rows, 2, 4 * HALF)
    grad_out = grad_heads[:, :, 3 * HALF :].reshape(rows, D)
    grad_qkv = grad_heads[:, :, : 3 * HALF].reshape(rows, 2, 2, 3, WIDTH)
    grad_qkv = grad_qkv.transpose(0, 3, 1, 2, 4).reshape(rows, 3 * D)
    pieces = (grad_qkv, grad_out, grad_in, grad_down, grad_vectors)
    local_square = sum(jnp.sum(piece * piece) for piece in pieces)
    norm = jnp.sqrt(links.total(jnp.broadcast_to(local_square, (8, 128)))[0, 0])
    clip = jnp.minimum(1.0, clip_limit / (norm + 1e-06))
    masters = (w_qkv, w_out, w_in, w_down, vectors)
    firsts = (first_qkv, first_out, first_in, first_down, first_vectors)
    seconds = (second_qkv, second_out, second_in, second_down, second_vectors)
    results = [
        adam_step(w, g, f, s, clip, float(STEPS))
        for w, g, f, s in zip(masters, pieces, firsts, seconds)
    ]
    return (output, input_grad, norm.reshape(1)) + pieces + tuple(
        result[at] for at in range(3) for result in results
    )


def solution(mesh):
    fsdp, rep = mesh.shape["fsdp"], mesh.shape["rep"]
    sizes = {"z": fsdp // 2, "y": 2, "x": rep // 2, "c": 2}
    cut = Mesh(mesh.devices.reshape(tuple(sizes.values())), tuple(sizes))
    names = tuple(sizes)
    wide, flat = P(names, None), P(names)
    group = (wide, wide, wide, wide, flat)
    body = jax.shard_map(
        functools.partial(per_device, Links(sizes)),
        mesh=cut,
        in_specs=(wide, wide, flat) + group * 3,
        out_specs=(wide, wide, P()) + group * 4,
        check_vma=False,
    )
    return body
```

```python
import functools
import math

import jax
import jax.numpy as jnp
from jax import lax
from jax.experimental import pallas as pl
from jax.experimental.pallas import tpu as pltpu
from jax.sharding import Mesh
from jax.sharding import PartitionSpec as P

D = 1024
FF = 4096
HEAD_DIM = 64
ROT = 16
STEPS = 10

first_decay = 0.9
second_decay = 0.95
adam_eps = 1e-08
weight_decay = 0.1
learn_rate = 0.02
clip_limit = 1.0
norm_eps = 1e-05

bf16 = jnp.bfloat16
f32 = jnp.float32

HEADS_STEP = 4
WIDTH = HEADS_STEP * HEAD_DIM
QUERY_ROWS = 256
FF_TILE = 512
TOKEN_TILE = 256
HALF = D // 2
VMEM_BYTES = 58 * 2**20


def mul(a, b, dim_a, dim_b):
    return lax.dot_general(a, b, (((dim_a,), (dim_b,)), ((), ())), preferred_element_type=f32)


def positions_of(segments):
    index = jnp.arange(segments.shape[0], dtype=jnp.int32)
    starts = jnp.concatenate([jnp.ones((1,), dtype=bool), segments[1:] != segments[:-1]])
    first = lax.cummax(jnp.where(starts, index, jnp.zeros_like(index)), axis=0)
    return index - first


def split_vector(vector):
    cuts = [3 * D, 4 * D, 4 * D + FF, 5 * D + FF, 6 * D + FF, 7 * D + FF, 8 * D + FF]
    return jnp.split(vector, cuts)


def adam_step(weight, grad, first, second, clip, count):
    scaled = grad * clip
    new_first = first_decay * first + (1.0 - first_decay) * scaled
    new_second = second_decay * second + (1.0 - second_decay) * scaled * scaled
    fix_one = 1.0 - first_decay**count
    fix_two = 1.0 - second_decay**count
    change = -learn_rate * (
        new_first / fix_one / (jnp.sqrt(new_second / fix_two) + adam_eps) + weight_decay * weight
    )
    return (new_first, new_second, change)


def call(kernel, grid, in_specs, out_specs, out_shape, args, after=(), scratch=(), aliases=None, flops=0, moved=0):
    count = len(args)

    def run(*refs):
        kernel(*refs[: 1 + count], *refs[1 + count + len(after) :])

    return pl.pallas_call(
        run,
        grid_spec=pltpu.PrefetchScalarGridSpec(
            num_scalar_prefetch=1,
            grid=grid,
            in_specs=list(in_specs) + [pl.BlockSpec(memory_space=pl.ANY)] * len(after),
            out_specs=list(out_specs),
            scratch_shapes=list(scratch),
        ),
        out_shape=list(out_shape),
        input_output_aliases=aliases or {},
        compiler_params=pltpu.CompilerParams(vmem_limit_bytes=VMEM_BYTES),
        cost_estimate=pl.CostEstimate(flops=flops, bytes_accessed=moved, transcendentals=0),
        name=kernel.__name__,
    )


def whole_block(shape):
    return pl.BlockSpec(shape, lambda g, core: (0,) * len(shape), pipeline_mode=pl.Buffered(1))


def by_core(core, near, far, axis):
    return jnp.where(
        core[0] == 0,
        jnp.concatenate([near, far], axis=axis),
        jnp.concatenate([far, near], axis=axis),
    )


def norm_kernel(core, tokens, gain_one, shift_one, gain_two, shift_two, na, nm, na_t, nm_t):
    inputs = tokens[...].astype(f32)
    centre = inputs - jnp.mean(inputs, axis=-1, keepdims=True)
    spread = jnp.mean(centre * centre, axis=-1, keepdims=True)
    normed = centre * lax.rsqrt(spread + norm_eps)
    one = (normed * gain_one[...] + shift_one[...]).astype(bf16)
    two = (normed * gain_two[...] + shift_two[...]).astype(bf16)
    na[...], nm[...], na_t[...], nm_t[...] = one, two, one.T, two.T


def norms(core, tokens, rows):
    length = tokens.shape[0]
    tile = pl.BlockSpec((TOKEN_TILE, D), lambda g, core: (g, 0))
    turned = pl.BlockSpec((D, TOKEN_TILE), lambda g, core: (0, g))
    sd = jax.ShapeDtypeStruct
    return call(
        norm_kernel, (length // TOKEN_TILE,), [tile] + [whole_block((1, D))] * 4,
        [tile, tile, turned, turned],
        [sd((length, D), bf16)] * 2 + [sd((D, length), bf16)] * 2,
        (tokens,) + rows, flops=10**7, moved=10**7,
    )(core, tokens, *rows)


def attention_kernel(core, start, cos, sin, na_t, cot, wq, wk, wv, wo, bq, bk, bv, *refs):
    refs, scratch = refs[:-7], refs[-7:]
    grads, merged, gq_out, gk_out, gv_out, sum_q, sum_k, sum_v = refs[-8:]
    bias, merged_t, gq_t, gk_t, gv_t, acc_k, acc_v = scratch
    length = cot.shape[0]

    @pl.when(pl.program_id(0) == 0)
    def _():
        key = lax.broadcasted_iota(jnp.int32, (length, length), 0)
        query = lax.broadcasted_iota(jnp.int32, (length, length), 1)
        bias[...] = jnp.where((key >= start[...]) & (key <= query), 0.0, -1e30)

    c, s = cos[...], sin[...]

    def project(w, b):
        return mul(w[...], na_t[...], 0, 0) + b[...]

    def rotate(v, sign):
        rows = []
        for h in range(HEADS_STEP):
            at = h * HEAD_DIM
            lo, hi = v[at : at + 8], v[at + 8 : at + 16]
            rows += [lo * c - sign * (hi * s), hi * c + sign * (lo * s), v[at + 16 : at + HEAD_DIM]]
        return jnp.concatenate(rows, axis=0)

    scale = HEAD_DIM**-0.5
    q_t = rotate(project(wq, bq), 1.0).astype(bf16) * jnp.asarray(scale, bf16)
    k_t = rotate(project(wk, bk), 1.0).astype(bf16)
    v_t = project(wv, bv).astype(bf16)
    gm_t = mul(wo[...], cot[...], 1, 1).astype(bf16)
    k, v = k_t.T, v_t.T
    for h in range(HEADS_STEP):
        hs = slice(h * HEAD_DIM, (h + 1) * HEAD_DIM)
        acc_k[...] = jnp.zeros_like(acc_k)
        acc_v[...] = jnp.zeros_like(acc_v)
        for i in range(length // QUERY_ROWS):
            n = QUERY_ROWS * (i + 1)
            qs = slice(i * QUERY_ROWS, n)
            scores = mul(k[:n, hs], q_t[hs, qs], 1, 0) + bias[:n, qs]
            weights = jnp.exp(scores - jnp.max(scores, axis=0, keepdims=True))
            probs = weights * (1.0 / jnp.sum(weights, axis=0, keepdims=True))
            probs_low = probs.astype(bf16)
            merged_t[hs, qs] = mul(v_t[hs, :n], probs_low, 1, 0).astype(bf16)
            grad_probs = mul(v[:n, hs], gm_t[hs, qs], 1, 0)
            inner = jnp.sum(grad_probs * probs, axis=0, keepdims=True)
            grad_scores = (probs * (grad_probs - inner)).astype(bf16)
            gq_t[hs, qs] = mul(k_t[hs, :n], grad_scores, 1, 0) * scale
            acc_k[:, :n] += mul(q_t[hs, qs], grad_scores, 1, 1)
            acc_v[:, :n] += mul(gm_t[hs, qs], probs_low, 1, 1)
        gk_t[hs, :] = acc_k[...]
        gv_t[hs, :] = acc_v[...]
    gq = rotate(gq_t[...], -1.0).astype(bf16)
    gk = rotate(gk_t[...], -1.0).astype(bf16)
    gv = gv_t[...].astype(bf16)
    merged[...], gq_out[...], gk_out[...], gv_out[...] = merged_t[...], gq, gk, gv
    for at, (part, out) in enumerate(((gq, sum_q), (gk, sum_k), (gv, sum_v))):
        out[...] = jnp.sum(part.astype(f32), axis=1, keepdims=True)
        grads[:, at * WIDTH : (at + 1) * WIDTH] = mul(na_t[...], part, 1, 1).astype(bf16)


def attention(core, own, part, parts, start, cos, sin, na_t, cot, weights, bias_qkv, before=(), grads=None):
    length = cot.shape[0]

    def at(core, g):
        return part + g + 2 * (core[0] if own else 1 - core[0])

    def columns(kind):
        return pl.BlockSpec((D, WIDTH), lambda g, core: (0, 4 * kind + at(core, g)))

    def entries(kind):
        return pl.BlockSpec((WIDTH, 1), lambda g, core: (4 * kind + at(core, g), 0))

    sd = jax.ShapeDtypeStruct
    args = (start, cos, sin, na_t, cot) + (weights,) * 4 + (bias_qkv,) * 3
    in_specs = [whole_block(a.shape) for a in args[:5]] + [columns(0), columns(1), columns(2)]
    in_specs += [pl.BlockSpec((WIDTH, D), lambda g, core: (at(core, g), 3))]
    in_specs += [entries(0), entries(1), entries(2)]
    out_specs = [pl.BlockSpec((D, 3 * WIDTH), lambda g, core: (0, part + g))]
    out_specs += [pl.BlockSpec((WIDTH, length), lambda g, core: (at(core, g), 0))] * 4
    out_specs += [entries(0)] * 3
    out_shape = [sd((D, 4 * HALF), bf16)] + [sd((D, length), bf16)] * 4 + [sd((D, 1), f32)] * 3
    kept = ((grads,) if grads is not None else ()) + tuple(before)
    first = 1 + len(args)
    return call(
        attention_kernel, (parts,), in_specs, out_specs, out_shape, args, kept,
        aliases={first + i: len(out_shape) - len(kept) + i for i in range(len(kept))},
        scratch=[
            pltpu.VMEM((length, length), f32),
            pltpu.VMEM((WIDTH, length), bf16),
            pltpu.VMEM((WIDTH, length), f32),
            pltpu.VMEM((WIDTH, length), f32),
            pltpu.VMEM((WIDTH, length), f32),
            pltpu.VMEM((HEAD_DIM, length), f32),
            pltpu.VMEM((HEAD_DIM, length), f32),
        ],
        flops=parts * 25 * 10**9, moved=2 * 10**7,
    )(core, *args, *kept)


def grad_out_kernel(core, merged, cot, far, near):
    grad = mul(merged[...], cot[...], 1, 0).astype(bf16)
    left = core[0] == 0
    far[...] = jnp.where(left, grad[:, HALF:], grad[:, :HALF])
    near[...] = jnp.where(left, grad[:, :HALF], grad[:, HALF:])


def grads_out(core, merged, cot, near):
    args = (merged, cot)
    rows = pl.BlockSpec((WIDTH, cot.shape[0]), lambda g, core: (g, 0))
    return call(
        grad_out_kernel, (D // WIDTH,), [rows, whole_block(cot.shape)],
        [
            pl.BlockSpec((WIDTH, HALF), lambda g, core: (g, 0)),
            pl.BlockSpec((WIDTH, HALF), lambda g, core: (g, 3)),
        ],
        [jax.ShapeDtypeStruct((D, HALF), bf16), jax.ShapeDtypeStruct(near.shape, bf16)],
        args, (near,), aliases={1 + len(args): 1}, flops=3 * 10**9, moved=10**7,
    )(core, *args, near)


def ffn_kernel(
    core, nm, cot, w_in, wd_near, wd_far, b_in, far, near, active_out, grad_out, grad_b
):
    w_down = by_core(core, wd_near[...], wd_far[...], 1)
    hidden = mul(nm[...], w_in[...], 1, 0) + b_in[...]
    cdf = 0.5 * (1.0 + lax.erf(hidden * (2.0**-0.5)))
    pdf = jnp.exp(-0.5 * hidden * hidden) * (1.0 / math.sqrt(2.0 * math.pi))
    active = (hidden * cdf).astype(bf16)
    grad_hidden = (mul(cot[...], w_down, 1, 1) * (cdf + hidden * pdf)).astype(bf16)
    active_out[...], grad_out[...] = active, grad_hidden
    grad_b[...] = jnp.sum(grad_hidden.astype(f32), axis=0, keepdims=True)
    grad_down = mul(active, cot[...], 0, 0).astype(bf16)
    left = core[0] == 0
    far[...] = jnp.where(left, grad_down[:, HALF:], grad_down[:, :HALF]).reshape(far.shape)
    near[...] = jnp.where(left, grad_down[:, :HALF], grad_down[:, HALF:]).reshape(near.shape)


def ffn(core, blocks, nm, cot, w_in, wd_near, wd_far, b_in):
    length = nm.shape[0]
    deep = FF // blocks
    share = pl.BlockSpec((FF_TILE // deep, deep, HALF), lambda g, core: (g, 0, 0))
    sd = jax.ShapeDtypeStruct
    columns = pl.BlockSpec((D, FF_TILE), lambda g, core: (0, g))
    tall = pl.BlockSpec((length, FF_TILE), lambda g, core: (0, g))
    row = pl.BlockSpec((1, FF_TILE), lambda g, core: (0, g))
    half = pl.BlockSpec((FF_TILE, HALF), lambda g, core: (g, 0))
    args = (nm, cot, w_in, wd_near, wd_far, b_in)
    return call(
        ffn_kernel, (FF // FF_TILE,),
        [whole_block((length, D))] * 2 + [columns, half, half, row],
        [share, share, tall, tall, row],
        [sd((blocks, 2 * deep, HALF), bf16)] * 2 + [sd((length, FF), bf16)] * 2 + [sd((1, FF), f32)],
        args, flops=30 * 10**9, moved=5 * 10**7,
    )(core, *args)


def grad_in_kernel(core, nm_t, grad_hidden, far, near):
    step = pl.program_id(0)
    half = pl.num_programs(0) // 2

    def store(ref):
        ref[...] = mul(nm_t[...], grad_hidden[...], 1, 0).astype(bf16).reshape(ref.shape)

    pl.when(step < half)(lambda: store(far))
    pl.when(step >= half)(lambda: store(near))


def grads_in(core, nm_t, grad_hidden, far, near):
    length = nm_t.shape[1]
    blocks = far.shape[0]
    half = FF // FF_TILE // 2
    split = (blocks, 2 * half, D // blocks, FF_TILE)
    args = (nm_t, grad_hidden)
    first = 1 + len(args)
    cut = (blocks, 1, D // blocks, FF_TILE)
    return call(
        grad_in_kernel, (2 * half,),
        [
            whole_block((D, length)),
            pl.BlockSpec(
                (length, FF_TILE), lambda g, core: (0, lax.rem(g + (1 - core[0]) * half, 2 * half))
            ),
        ],
        [
            pl.BlockSpec(cut, lambda g, core: (0, half + jnp.minimum(g, half - 1), 0, 0)),
            pl.BlockSpec(cut, lambda g, core: (0, half + jnp.maximum(g - half, 0), 0, 0)),
        ],
        [jax.ShapeDtypeStruct(split, bf16)] * 2, args, (far.reshape(split), near.reshape(split)),
        aliases={first: 0, first + 1: 1}, flops=9 * 10**9, moved=2 * 10**7,
    )(core, *args, far.reshape(split), near.reshape(split))


def output_kernel(core, tokens, merged, active, wo, wd_near, wd_far, b_sum, output):
    att = mul(merged[...], wo[...], 0, 0)
    fed = by_core(
        core, mul(active[...], wd_near[...], 1, 0), mul(active[...], wd_far[...], 1, 0), 1
    )
    output[...] = (tokens[...].astype(f32) + att + fed + b_sum[...]).astype(bf16)


def outputs(core, tokens, merged, active, weights, wd_near, wd_far, b_sum, after):
    length = tokens.shape[0]
    tile = pl.BlockSpec((TOKEN_TILE, D), lambda g, core: (g, 0))
    turned = pl.BlockSpec((D, TOKEN_TILE), lambda g, core: (0, g))
    w_out = pl.BlockSpec((D, D), lambda g, core: (0, 3), pipeline_mode=pl.Buffered(1))
    args = (tokens, merged, active, weights, wd_near, wd_far, b_sum)
    return call(
        output_kernel, (length // TOKEN_TILE,),
        [tile, turned, pl.BlockSpec((TOKEN_TILE, FF), lambda g, core: (g, 0)), w_out]
        + [whole_block((FF, HALF))] * 2 + [whole_block((1, D))],
        [tile], [jax.ShapeDtypeStruct((length, D), bf16)], args, after,
        flops=11 * 10**9, moved=3 * 10**7,
    )(core, *args, *after)[0]


def grad_normed_kernel(core, grad_hidden, w_in, grad_nm):
    grad_nm[...] = mul(grad_hidden[...], w_in[...], 1, 1)


def grads_normed(core, grad_hidden, w_in):
    length = grad_hidden.shape[0]
    return call(
        grad_normed_kernel, (length // TOKEN_TILE,),
        [
            pl.BlockSpec((TOKEN_TILE, FF), lambda g, core: (g, 0)),
            pl.BlockSpec((D, FF), lambda g, core: (0, 0), pipeline_mode=pl.Buffered(1)),
        ],
        [pl.BlockSpec((TOKEN_TILE, D), lambda g, core: (g, 0))],
        [jax.ShapeDtypeStruct((length, D), f32)], (grad_hidden, w_in),
        flops=9 * 10**9, moved=2 * 10**7,
    )(core, grad_hidden, w_in)[0]


def input_kernel(
    core, tokens, cot, gq, gk, gv, grad_nm, w_qkv, gain_one, gain_two, input_grad, sums
):
    inputs = tokens[...].astype(f32)
    centre = inputs - jnp.mean(inputs, axis=-1, keepdims=True)
    spread = jnp.mean(centre * centre, axis=-1, keepdims=True)
    rstd = lax.rsqrt(spread + norm_eps)
    normed = centre * rstd
    joined = jnp.concatenate([gq[...], gk[...], gv[...]], axis=0)
    grad_na = mul(joined, w_qkv[...], 0, 1)
    grad_nm = grad_nm[...]
    grad_normed = grad_na * gain_one[...] + grad_nm * gain_two[...]
    cotangent = cot[...].astype(f32)
    input_grad[...] = cotangent + rstd * (
        grad_normed
        - jnp.mean(grad_normed, axis=-1, keepdims=True)
        - normed * jnp.mean(grad_normed * normed, axis=-1, keepdims=True)
    )

    @pl.when(pl.program_id(0) == 0)
    def _():
        sums[...] = jnp.zeros_like(sums)

    for at, terms in enumerate((cotangent, grad_na * normed, grad_na, grad_nm * normed, grad_nm)):
        sums[at : at + 1, :] += jnp.sum(terms, axis=0, keepdims=True)


def input_grads(core, tokens, cot, joined, grad_nm, weights, gains, after):
    length = tokens.shape[0]
    tile = pl.BlockSpec((TOKEN_TILE, D), lambda g, core: (g, 0))
    turned = pl.BlockSpec((D, TOKEN_TILE), lambda g, core: (0, g))
    once = functools.partial(pl.BlockSpec, pipeline_mode=pl.Buffered(1))
    args = (tokens, cot) + joined + (grad_nm, weights) + gains
    sd = jax.ShapeDtypeStruct
    return call(
        input_kernel, (length // TOKEN_TILE,),
        [tile, tile] + [turned] * 3 + [tile, once((D, 3 * D), lambda g, core: (0, 0))]
        + [whole_block((1, D))] * 2,
        [tile, whole_block((8, D))],
        [sd((length, D), f32), sd((8, D), f32)], args, after, flops=15 * 10**9, moved=4 * 10**7,
    )(core, *args, *after)


def round_kernel(core, value, low):
    low[...] = value[...].astype(bf16)


def rounded(core, value, after):
    block = whole_block(value.shape)
    low = jax.ShapeDtypeStruct(value.shape, bf16)
    return call(round_kernel, (1,), [block], [block], [low], (value,), after)(core, value, *after)[0]


def later(value, *after):
    return lax.optimization_barrier((value,) + after)[0]


class Links:
    def __init__(self, sizes):
        self.sizes = sizes
        self.nz = sizes["z"]
        self.every = tuple(sizes)

    def swap(self, axis, value, bit=1):
        return lax.ppermute(value, axis, [(i, i ^ bit) for i in range(self.sizes[axis])])

    def bits(self, axis):
        return [1 << i for i in range(self.sizes[axis].bit_length() - 1)]

    def total(self, value):
        for axis in self.every[::-1]:
            for bit in self.bits(axis):
                value = value + self.swap(axis, value, bit)
        return value

    def gather(self, value):
        x, y, z = (lax.axis_index(axis) for axis in "xyz")

        def ordered(at, own, other):
            return jnp.where(
                at == 0, jnp.concatenate([own, other]), jnp.concatenate([other, own])
            )

        column = value[None]
        for bit in self.bits("z")[:-1]:
            column = ordered(z // (2 * bit) % 2, column, self.swap("z", column, 2 * bit))
        other = self.swap("z", column)
        self.column = other
        even = jnp.where(z % 2 == 0, column, other)[:, None, None, None]
        odd = jnp.where(z % 2 == 0, other, column)[:, None, None, None]
        even_y, odd_x = self.swap("y", even), self.swap("x", odd)
        even = jnp.where(
            y == 0, jnp.concatenate([even, even_y], 2), jnp.concatenate([even_y, even], 2)
        )
        odd = jnp.where(
            x == 0, jnp.concatenate([odd, odd_x], 3), jnp.concatenate([odd_x, odd], 3)
        )
        even_x, odd_y = self.swap("x", even), self.swap("y", odd)
        whole = jnp.zeros((self.nz // 2, 2, 2, 2) + value.shape, value.dtype)
        for part, at in (
            (even, (0, 0, x)), (even_x, (0, 0, 1 - x)), (odd, (1, y, 0)), (odd_y, (1, 1 - y, 0))
        ):
            whole = lax.dynamic_update_slice(whole, part, (0,) + at + (0, 0))
        return whole.reshape(-1, value.shape[-1])

    def owners(self, held, core):
        rows = held.shape[0] // 2
        mine = lax.dynamic_slice_in_dim(held, core * rows, rows)
        came = self.swap("c", lax.dynamic_slice_in_dim(held, (1 - core) * rows, rows))
        return jnp.concatenate(
            [jnp.where(core == 0, mine, came), jnp.where(core == 0, came, mine)], axis=1
        )


class Scatter:
    def __init__(self, links, near, came):
        self.links, split = links, (links.nz // 2, 2, 2, 2, -1, near.shape[-1])
        self.near, self.came = near.reshape(split), came.reshape(split)
        self.x, self.y, self.z = (lax.axis_index(axis) for axis in "xyz")
        self.first = (
            self.term(0, x=1 - self.x).astype(bf16),
            self.term(1, y=1 - self.y).astype(bf16),
        )

    def term(self, odd, y=None, x=None):
        _, _, _, _, rows, n = self.near.shape
        size = (self.links.nz // 2, 1, 1 if y is not None else 2, 1 if x is not None else 2, rows, n)
        start = (0, odd, 0 if y is None else y, 0 if x is None else x, 0, 0)
        shape = tuple(count for at, count in enumerate(size) if at in (0, 4, 5) or count == 2)

        def cut(v):
            return lax.dynamic_slice(v, start, size).reshape(shape).astype(f32)

        return cut(self.near) + cut(self.came)

    def came_at(self, part, at):
        return lax.dynamic_index_in_dim(part, at, 1, False).astype(f32)

    def step_one(self, *after):
        even, odd = self.links.swap("x", self.first[0]), self.links.swap("y", self.first[1])
        self.even, self.odd = later((even, odd), *after)
        x, y = self.x, self.y
        self.second = (
            (self.term(0, 1 - y, x) + self.came_at(self.even, 1 - y)).astype(bf16),
            (self.term(1, y, 1 - x) + self.came_at(self.odd, 1 - x)).astype(bf16),
        )

    def step_two(self, *after):
        even, odd = self.links.swap("y", self.second[0]), self.links.swap("x", self.second[1])
        even, odd = later((even, odd), *after)
        x, y = self.x, self.y
        even = self.term(0, y, x) + self.came_at(self.even, y) + even.astype(f32)
        odd = self.term(1, y, x) + self.came_at(self.odd, x) + odd.astype(f32)
        low = self.z % 2 == 0
        self.keep, self.send = jnp.where(low, even, odd), jnp.where(low, odd, even).astype(bf16)

        self.bits = [1] + [2 * bit for bit in self.links.bits("z")[:-1]][::-1]

    def advance(self, *after):
        came = self.links.swap("z", self.send, self.bits.pop(0))
        self.held = self.keep + (later(came, *after) if after else came).astype(f32)
        if self.bits:
            bit = self.bits[0]
            mine, size = self.z // bit % 2, bit // 2
            self.send = lax.dynamic_slice_in_dim(self.held, (1 - mine) * size, size).astype(bf16)
            self.keep = lax.dynamic_slice_in_dim(self.held, mine * size, size)

    def finish(self):
        while self.bits:
            self.advance()
        return self.held[0]


def per_device(
    links,
    tokens,
    cotangent,
    doc_ids,
    w_qkv,
    w_out,
    w_in,
    w_down,
    vectors,
    first_qkv,
    first_out,
    first_in,
    first_down,
    first_vectors,
    second_qkv,
    second_out,
    second_in,
    second_down,
    second_vectors,
):
    every = links.every
    core = lax.axis_index("c")
    core_ref = core.astype(jnp.int32).reshape(1)
    length = tokens.shape[0]
    rows = w_qkv.shape[0]
    per_row = vectors.shape[0] // rows

    spare = jnp.pad(vectors.reshape(rows, per_row), ((0, 0), (0, 128 - per_row)))
    w_in_all = lax.all_gather(
        jnp.concatenate([w_in, spare], axis=1).astype(bf16), every, axis=0, tiled=True
    )
    halves = w_down.astype(bf16).reshape(-1, 2, HALF)
    mine = lax.dynamic_index_in_dim(halves, core, 1, False)
    came = links.swap("c", lax.dynamic_index_in_dim(halves, 1 - core, 1, False))
    wd_near = links.gather(
        jnp.where(core == 0, jnp.concatenate([mine, came]), jnp.concatenate([came, mine]))
    )
    wd_far = links.swap("c", wd_near)
    weights = lax.all_gather(
        rounded(core_ref, jnp.concatenate([w_qkv, w_out], axis=1), (links.column,)),
        every, axis=0, tiled=True,
    )
    vector_all = w_in_all[:, FF : FF + per_row].reshape(-1).astype(f32)
    b_qkv, b_out, b_in, b_down, gain_one, shift_one, gain_two, shift_two = split_vector(vector_all)

    positions = positions_of(doc_ids)
    start = (jnp.arange(length, dtype=jnp.int32) - positions).reshape(1, length)
    freqs = jnp.exp(jnp.arange(ROT // 2, dtype=f32) * (-2.0 * math.log(10000.0) / ROT))
    angles = freqs[:, None] * positions.astype(f32)[None, :]
    gains = (gain_one.reshape(1, D), gain_two.reshape(1, D))
    na, nm, na_t, nm_t = norms(
        core_ref, tokens, (gains[0], shift_one.reshape(1, D), gains[1], shift_two.reshape(1, D))
    )
    cos, sin = jnp.cos(angles), jnp.sin(angles)
    bias_qkv = b_qkv.reshape(3 * D, 1)
    blocks = D // rows // 2
    far, near, active, grad_hidden, sum_in = ffn(
        core_ref, blocks, nm, cotangent, w_in_all, wd_near, wd_far, b_in.reshape(1, FF)
    )
    far, near = grads_in(core_ref, nm_t, grad_hidden, far, near)
    deep = 2 * FF // blocks
    grad_nm = grads_normed(core_ref, later(grad_hidden, far), w_in_all)
    came_hidden = later(links.swap("c", far), grad_nm)
    hidden = Scatter(
        links, near.reshape(blocks * deep, HALF), came_hidden.reshape(blocks * deep, HALF)
    )
    heads = functools.partial(attention, core_ref)

    def common(*after):
        first = later(start, *after) if after else start
        return (first, cos, sin, na_t, cotangent, weights, bias_qkv)

    far, *kept = heads(False, 0, 1, *common(*hidden.first))
    far, *kept = heads(False, 1, 1, *common(), kept, far)
    came_heads = links.swap("c", far)
    hidden.step_one(kept[4])
    near, *kept = heads(True, 0, 1, *common(*hidden.second), kept)
    hidden.step_two(kept[4])
    near, *kept = heads(True, 1, 1, *common(hidden.send), kept, near)
    merged, *joined = kept[:4]
    out_far, near = grads_out(core_ref, merged, cotangent, near)
    came_out = links.swap("c", out_far)
    last = Scatter(
        links, near, lax.dynamic_update_slice(came_heads, came_out, (0, 3 * HALF))
    )
    output = outputs(
        core_ref, later(tokens, *last.first), merged, active, weights, wd_near, wd_far,
        (b_out + b_down).reshape(1, D), (),
    )
    last.step_one(output)
    hidden.advance(output)
    input_grad, sums = input_grads(
        core_ref, later(tokens, *last.second, hidden.send), cotangent, tuple(joined), grad_nm, weights, gains,
        (output,),
    )
    hidden.advance(sums)
    held = hidden.finish()
    deep = deep // 2
    held = jnp.concatenate(
        [
            held[:deep].reshape(2, deep // 2, HALF),
            held[deep:].reshape(-1, 2, rows, HALF).transpose(1, 0, 2, 3).reshape(2, -1, HALF),
        ],
        axis=1,
    ).reshape(-1, HALF)
    grad_rows = links.owners(held, core)
    grad_down = grad_rows[: deep // 2]
    grad_in = grad_rows[deep // 2 :].reshape(-1, rows, 2, HALF).transpose(1, 2, 0, 3).reshape(rows, FF)
    last.step_two(sums)
    vector_terms = jnp.concatenate(
        [part[:, 0] for part in kept[4:]] + [sums[0], sum_in[0], sums[0], sums[1], sums[2], sums[3], sums[4]]
    )
    vector_total = links.total(later(vector_terms, last.send).reshape(-1, 128)).reshape(-1)
    count_own = vectors.shape[0]
    grad_vectors = lax.dynamic_slice_in_dim(
        vector_total, lax.axis_index(every) * count_own, count_own
    )
    grad_heads = links.owners(last.finish(), core).reshape(rows, 2, 4 * HALF)
    grad_out = grad_heads[:, :, 3 * HALF :].reshape(rows, D)
    grad_qkv = grad_heads[:, :, : 3 * HALF].reshape(rows, 2, 2, 3, WIDTH)
    grad_qkv = grad_qkv.transpose(0, 3, 1, 2, 4).reshape(rows, 3 * D)
    pieces = (grad_qkv, grad_out, grad_in, grad_down, grad_vectors)
    local_square = sum(jnp.sum(piece * piece) for piece in pieces)
    norm = jnp.sqrt(links.total(jnp.broadcast_to(local_square, (8, 128)))[0, 0])
    clip = jnp.minimum(1.0, clip_limit / (norm + 1e-06))
    masters = (w_qkv, w_out, w_in, w_down, vectors)
    firsts = (first_qkv, first_out, first_in, first_down, first_vectors)
    seconds = (second_qkv, second_out, second_in, second_down, second_vectors)
    results = [
        adam_step(w, g, f, s, clip, float(STEPS))
        for w, g, f, s in zip(masters, pieces, firsts, seconds)
    ]
    return (output, input_grad, norm.reshape(1)) + pieces + tuple(
        result[at] for at in range(3) for result in results
    )


def solution(mesh):
    fsdp, rep = mesh.shape["fsdp"], mesh.shape["rep"]
    sizes = {"z": fsdp // 2, "y": 2, "x": rep // 2, "c": 2}
    cut = Mesh(mesh.devices.reshape(tuple(sizes.values())), tuple(sizes))
    names = tuple(sizes)
    wide, flat = P(names, None), P(names)
    group = (wide, wide, wide, wide, flat)
    body = jax.shard_map(
        functools.partial(per_device, Links(sizes)),
        mesh=cut,
        in_specs=(wide, wide, flat) + group * 3,
        out_specs=(wide, wide, P()) + group * 4,
        check_vma=False,
    )
    return body
```
